32 devices in a mesh: seq: 8 (over z, x), head: 2 (over y), pair: 2 (over core).
Axes of the slice: x: 2, y: 2, z: 4, core: 2. Of those that a mesh axis runs over, the one named last changes fastest.
Arguments:
- queries: bfloat16 [6144, 5120], P(('pair', 'seq'), 'head'), parts along dimension 0, may hold values from -12 to 12
- keys: bfloat16 [6144, 5120], P(('pair', 'seq'), 'head'), parts along dimension 0, may hold values from -12 to 12
- values: bfloat16 [6144, 5120], P(('pair', 'seq'), 'head'), parts along dimension 0, may hold values from -6 to 6
- cross_query: bfloat16 [6144, 5120], P(('pair', 'seq'), 'head'), parts along dimension 0, may hold values from -12 to 12
- text_keys: bfloat16 [1024, 5120], P('pair', 'head'), parts along dimension 0, may hold values from -12 to 12
- text_values: bfloat16 [1024, 5120], P('pair', 'head'), parts along dimension 0, may hold values from -6 to 6
- out_weight: bfloat16 [5120, 5120], P('head'), may hold values from -0.078125 to 0.078125
- block_list: int32 [24, 18], replicated, may hold values from 0 to 23, as said below
- block_count: int32 [24], replicated, may hold values from 6 to 18, as said below
Outputs:
- block_stream: bfloat16 [6144, 5120], P(('pair', 'seq'), 'head'), parts along dimension 0
- cross_heads: bfloat16 [6144, 5120], P(('pair', 'seq'), 'head'), parts along dimension 0
The draws below stay inside these ranges and needn't reach their ends.
There are 2 independent parts, one for each index of `pair`. The reference program is written for one: setup_inputs(seed, part) draws one part's arguments, and reference() takes and returns one part's arrays. A program takes and returns all parts, laid end to end along the dimension named above; an argument that names none is the same for every part. Nothing has to cross between parts.
Inputs may be any that keep to these rules, and one draw needn't show every extreme that they name: `block_list`: each row holds 18 distinct key blocks; its first block_count entries include every block of frame groups f - 1, f and f + 1 (those that exist) and of group 0, with f = row // 3 and a frame group being 3 consecutive blocks. `block_count`: some row uses all 18 entries.
All inputs are finite; a program needn't handle non-finite values.
Results may differ from the reference program's by a relative error of at most 0.029.
Values may be sent and summed in bfloat16 or wider, within the bound.
A program may use at most 192 MiB of HBM per device.

```python
import jax
import jax.numpy as jnp
from jax import lax

D = 5120
HEADS = 40
DH = 128
TEXT = 512
BLK = 128
FB = 3
KB = 24
NB = 18
S = 3072
HD = 5120
N_HEAD = 2


def base_draw(key, salt, count):
    return jax.random.normal(jax.random.fold_in(key, salt), (count, HEADS * DH))


def draw_queries(key, part):
    field = base_draw(key, 10, S)
    return field.astype(jnp.bfloat16)


def draw_keys(key, part):
    field = base_draw(key, 11, S)
    return field.astype(jnp.bfloat16)


def draw_cross_query(key, part):
    field = base_draw(key, 12, S)
    return field.astype(jnp.bfloat16)


def draw_text_keys(key, part):
    field = base_draw(key, 13, TEXT)
    return field.astype(jnp.bfloat16)


def mask_parts(key):
    blocks = jnp.arange(KB, dtype=jnp.int32)
    frame = blocks // FB
    needed = (jnp.abs(frame[:, None] - frame[None, :]) <= 1) | (frame[None, :] == 0)
    noise = jax.random.randint(jax.random.fold_in(key, 21), (KB, KB), 0, 4096)
    scored = (noise + 8192 * needed.astype(jnp.int32)) * KB + blocks[None, :]
    unused, picked = lax.top_k(scored, NB)
    needed_count = jnp.sum(needed.astype(jnp.int32), axis=1)
    extra = jax.random.randint(jax.random.fold_in(key, 22), (KB,), 0, NB + 1 - needed_count)
    count = needed_count + extra
    fullest = jax.random.randint(jax.random.fold_in(key, 23), (), 0, KB)
    count = jnp.where(blocks == fullest, NB, count)
    return (picked.astype(jnp.int32), count.astype(jnp.int32))


def draw_block_list(key, part):
    return mask_parts(key)[0]


def draw_block_count(key, part):
    return mask_parts(key)[1]


def levels(rng, shape, pieces, smallest, top_value):
    loudness, own = 1.0, jax.random.fold_in(rng, 6)
    for position, shards_of in pieces:
        draws = jnp.exp(jax.random.uniform(jax.random.fold_in(own, position), (shards_of,), jnp.float32, smallest / len(pieces), top_value / len(pieces)))
        loudness = loudness * jnp.repeat(draws, shape[position] // shards_of).reshape([-1 if axis == position else 1 for axis in range(len(shape))])
    return loudness


def gaussian(own_key, dims, spread, bound, cuts=(), kind=jnp.bfloat16):
    level = levels(own_key, dims, cuts, -0.22, 0.18) if cuts else 1.0
    drawn = jax.random.normal(own_key, dims, jnp.float32) * spread * level
    return jnp.minimum(jnp.maximum(drawn, -bound), bound).astype(kind)


def setup_inputs(seed: int = 0, part: int = 0) -> dict:
    streams_of = jax.random.split(jax.random.key(seed), 10)
    own_keys = jax.random.split(jax.random.fold_in(streams_of[9], part), 10)
    queries = draw_queries(jax.random.fold_in(jax.random.fold_in(streams_of[9], part), 71), part)
    keys = draw_keys(jax.random.fold_in(jax.random.fold_in(streams_of[9], part), 71), part)
    values = gaussian(own_keys[2], (S, HD), 1.0, 6.0, ((0, 8), (1, 2)))
    cross_query = draw_cross_query(jax.random.fold_in(jax.random.fold_in(streams_of[9], part), 71), part)
    text_keys = draw_text_keys(jax.random.fold_in(jax.random.fold_in(streams_of[9], part), 71), part)
    text_values = gaussian(own_keys[5], (TEXT, HD), 1.0, 6.0, ((1, 2),))
    out_weight = gaussian(streams_of[6], (HD, D), HD ** -0.5, 0.078125, ((0, 2),))
    block_list = draw_block_list(jax.random.fold_in(streams_of[9], 71), part)
    block_count = draw_block_count(jax.random.fold_in(streams_of[9], 71), part)
    return {"queries": queries, "keys": keys, "values": values, "cross_query": cross_query, "text_keys": text_keys, "text_values": text_values, "out_weight": out_weight, "block_list": block_list, "block_count": block_count}


def allowed_table(block_list, block_count):
    slots = jnp.arange(block_list.shape[1], dtype=jnp.int32)
    targets = jnp.arange(block_list.shape[0], dtype=jnp.int32)
    hit = (block_list[:, :, None] == targets[None, None, :]) & (slots[None, :, None] < block_count[:, None, None])
    return jnp.any(hit, axis=1).astype(jnp.int32)


def attend_head(query_head, key_head, value_head, token_mask, scale):
    score = jnp.dot(query_head, key_head.T, preferred_element_type=jnp.float32) * scale
    score = jnp.where(token_mask, score, -1e30)
    row_max = jnp.max(score, axis=1, keepdims=True)
    weight = jnp.where(token_mask, jnp.exp(score - row_max), 0.0)
    total = jnp.sum(weight, axis=1, keepdims=True)
    summed = jnp.dot(weight.astype(jnp.bfloat16), value_head, preferred_element_type=jnp.float32)
    return summed / total


def split_heads(array):
    return array.reshape(array.shape[0], HEADS, DH).transpose(1, 0, 2)


def reference(queries, keys, values, cross_query, text_keys, text_values, out_weight, block_list, block_count):
    scale = DH ** -0.5
    allowed = allowed_table(block_list, block_count) > 0
    token_mask = jnp.repeat(jnp.repeat(allowed, BLK, axis=0), BLK, axis=1)

    def self_head(items):
        return attend_head(items[0], items[1], items[2], token_mask, scale)

    self_out = lax.map(self_head, (split_heads(queries), split_heads(keys), split_heads(values)))
    self_heads = self_out.transpose(1, 0, 2).reshape(S, HD).astype(jnp.bfloat16)

    text_mask = jnp.ones((S, TEXT), dtype=bool)

    def cross_head(items):
        return attend_head(items[0], items[1], items[2], text_mask, scale)

    cross_out = lax.map(cross_head, (split_heads(cross_query), split_heads(text_keys), split_heads(text_values)))
    cross_heads = cross_out.transpose(1, 0, 2).reshape(S, HD).astype(jnp.bfloat16)

    group = HD // N_HEAD
    stream = jnp.zeros((S, D), jnp.float32)
    for index in range(N_HEAD):
        partial_sum = jnp.dot(self_heads[:, index * group:(index + 1) * group], out_weight[index * group:(index + 1) * group], preferred_element_type=jnp.float32)
        partial_sum = lax.optimization_barrier(partial_sum.astype(jnp.bfloat16)).astype(jnp.float32)
        stream = stream + partial_sum
    return stream.astype(jnp.bfloat16), cross_heads
```

```python
import functools

import jax
import jax.numpy as jnp
from jax import lax
from jax.experimental import pallas as pl
from jax.experimental.pallas import tpu as pltpu
from jax.sharding import PartitionSpec as P

DH = 128
BLK = 128


def allowed_table(block_list, block_count):
    slots = jnp.arange(block_list.shape[1], dtype=jnp.int32)
    targets = jnp.arange(block_list.shape[0], dtype=jnp.int32)
    hit = (block_list[:, :, None] == targets[None, None, :]) & (
        slots[None, :, None] < block_count[:, None, None]
    )
    return jnp.any(hit, axis=1).astype(jnp.int32)


def attend_tile(carry, query_three, key_tile, value_tile, tile_mask, scale):
    row_max, total, summed = carry
    count = key_tile.shape[0]
    heads_here = query_three.shape[1]
    key_three = key_tile.reshape(count, heads_here, DH)
    value_three = value_tile.reshape(count, heads_here, DH)
    score = (
        jnp.einsum("qhd,khd->hqk", query_three, key_three, preferred_element_type=jnp.float32)
        * scale
    )
    score = jnp.where(tile_mask[None], score, -1e30)
    new_max = jnp.maximum(row_max, jnp.max(score, axis=2))
    weight = jnp.where(tile_mask[None], jnp.exp(score - new_max[:, :, None]), 0.0)
    factor = jnp.exp(row_max - new_max)
    total = total * factor + jnp.sum(weight, axis=2)
    update = jnp.einsum(
        "hqk,khd->hqd", weight.astype(jnp.bfloat16), value_three, preferred_element_type=jnp.float32
    )
    summed = summed * factor[:, :, None] + update
    return (new_max, total, summed)


def masked_update(carry, query_three, key_tile, value_tile, tile_mask, scale):
    return attend_tile(carry, query_three, key_tile, value_tile, tile_mask, scale)


def empty_state(heads_here, count):
    return (
        jnp.full((heads_here, count), -1e30, jnp.float32),
        jnp.zeros((heads_here, count), jnp.float32),
        jnp.zeros((heads_here, count, DH), jnp.float32),
    )


def body(
    queries, keys, values, cross_query, text_keys, text_values, out_weight, block_list, block_count
):
    scale = DH ** (-0.5)
    rows = queries.shape[0]
    heads_here = queries.shape[1] // DH
    blocks_here = rows // BLK
    allowed = allowed_table(block_list, block_count) > 0
    my_first = lax.axis_index("seq") * blocks_here
    query_three = queries.reshape(rows, heads_here, DH)
    row_allowed = jnp.repeat(
        lax.dynamic_slice_in_dim(allowed, my_first, blocks_here, 0), BLK, axis=0
    )
    key_piece = lax.all_gather(keys, "seq", axis=0, tiled=True)
    value_piece = lax.all_gather(values, "seq", axis=0, tiled=True)
    count = key_piece.shape[0]
    shards_in = count // rows
    factor = 1
    for candidate in range(1, shards_in + 1):
        if shards_in % candidate == 0 and candidate * rows <= 1536:
            factor = candidate
    width = factor * rows
    piece_mask = jnp.repeat(row_allowed, BLK, axis=1)
    tiles = count // width
    key_tiles = key_piece.reshape(tiles, width, key_piece.shape[1])
    value_tiles = value_piece.reshape(tiles, width, value_piece.shape[1])
    mask_tiles = piece_mask.reshape(rows, tiles, width).transpose(1, 0, 2)

    def step(state, items):
        return (masked_update(state, query_three, items[0], items[1], items[2], scale), None)

    state, unused = lax.scan(
        step, empty_state(heads_here, rows), (key_tiles, value_tiles, mask_tiles)
    )
    row_max, total, summed = state
    self_three = (summed / total[:, :, None]).transpose(1, 0, 2)
    self_heads = self_three.reshape(rows, heads_here * DH).astype(jnp.bfloat16)
    term = jnp.dot(self_heads, out_weight, preferred_element_type=jnp.float32)
    block_stream = lax.psum_scatter(
        term.astype(jnp.bfloat16), "head", scatter_dimension=1, tiled=True
    )
    cross_three = cross_query.reshape(rows, heads_here, DH)
    text_count = text_keys.shape[0]
    text_key_three = text_keys.reshape(text_count, heads_here, DH)
    text_value_three = text_values.reshape(text_count, heads_here, DH)
    cross_score = (
        jnp.einsum("qhd,khd->hqk", cross_three, text_key_three, preferred_element_type=jnp.float32)
        * scale
    )
    cross_max = jnp.max(cross_score, axis=2, keepdims=True)
    cross_weight = jnp.exp(cross_score - cross_max)
    cross_total = jnp.sum(cross_weight, axis=2)
    cross_sum = jnp.einsum(
        "hqk,khd->hqd",
        cross_weight.astype(jnp.bfloat16),
        text_value_three,
        preferred_element_type=jnp.float32,
    )
    cross_heads = (
        (cross_sum / cross_total[:, :, None])
        .transpose(1, 0, 2)
        .reshape(rows, heads_here * DH)
        .astype(jnp.bfloat16)
    )
    return (block_stream, cross_heads)


def fused_kernel(
    sizes,
    q_ref, k_ref, v_ref, cq_ref, tk_ref, tv_ref, w_ref, list_ref, count_ref,
    out_ref, cross_ref,
    kbuf, vbuf, qbuf, obuf, oin, wbuf, mine, ysend, yrecv, bias, cqb, tkb, tvb, cob,
    kv_send, kv_recv, x_send, x_recv, q_send, q_recv, o_send, o_recv, y_send, y_recv, own_sem, own_q, own_o, c_sem, out_sem,
):
    nz, rows, group, text, slots = sizes
    wide = group * DH
    blocks = rows // BLK
    chunk = nz * BLK
    half = out_ref.shape[1]
    seq = lax.axis_index("seq")
    z, x = seq // 2, lax.rem(seq, 2)
    y = lax.axis_index("head")
    factor = (DH ** (-0.5)) * 1.4426950408889634

    def at_z(zz):
        return {"seq": zz * 2 + x}

    def up(j):
        return lax.rem(z + j, nz)

    def down(j):
        return lax.rem(z + nz - j, nz)

    x_peer = {"seq": z * 2 + 1 - x}
    y_peer = {"head": 1 - y}

    def span(i, size):
        return pl.ds(pl.multiple_of(i * size, size), size)

    def remote(src, dst, send, recv, where):
        return pltpu.make_async_remote_copy(
            src_ref=src, dst_ref=dst, send_sem=send, recv_sem=recv,
            device_id=where, device_id_type=pl.DeviceIdType.MESH,
        )

    def frame(zz, xx):
        return span(zz * 2 + xx, rows)

    own_w = pltpu.make_async_copy(w_ref, wbuf, own_sem.at[2])
    own_w.start()

    barrier = pltpu.get_barrier_semaphore()
    for j in range(1, nz):
        pl.semaphore_signal(barrier, inc=1, device_id=at_z(up(j)), device_id_type=pl.DeviceIdType.MESH)
    pl.semaphore_signal(barrier, inc=1, device_id=x_peer, device_id_type=pl.DeviceIdType.MESH)
    pl.semaphore_signal(barrier, inc=1, device_id=y_peer, device_id_type=pl.DeviceIdType.MESH)
    pl.semaphore_wait(barrier, nz + 1)

    pairs = ((k_ref, kbuf), (v_ref, vbuf))

    def kv_copy(a, j):
        return remote(pairs[a][0].at[:, span(up(j), wide)], pairs[a][1].at[frame(z, x), :],
                      kv_send.at[a, j], kv_recv.at[a, j], at_z(up(j)))

    def kv_landing(a, j):
        place = pairs[a][1].at[frame(down(j), x), :]
        return remote(place, place, kv_send.at[a, j], kv_recv.at[a, j], at_z(down(j)))

    def x_copy(a, j):
        place = pairs[a][1].at[frame(down(j), x), :]
        source = place if j else pairs[a][0].at[:, span(z, wide)]
        return remote(source, place, x_send.at[a, j], x_recv.at[a, j], x_peer)

    def x_landing(a, j):
        place = pairs[a][1].at[frame(down(j), 1 - x), :]
        return remote(place, place, x_send.at[a, j], x_recv.at[a, j], x_peer)

    def q_copy(c, j):
        return remote(q_ref.at[span(c, BLK), span(up(j), wide)], qbuf.at[span(c * nz + z, BLK), :],
                      q_send.at[c, j], q_recv.at[c, j], at_z(up(j)))

    def q_landing(c, j):
        place = qbuf.at[span(c * nz + down(j), BLK), :]
        return remote(place, place, q_send.at[c, j], q_recv.at[c, j], at_z(down(j)))

    def o_copy(c, j):
        return remote(obuf.at[span(c * nz + up(j), BLK), :], oin.at[span(c, BLK), span(z, wide)],
                      o_send.at[c, j], o_recv.at[c, j], at_z(up(j)))

    def o_landing(c, j):
        place = oin.at[span(c, BLK), span(down(j), wide)]
        return remote(place, place, o_send.at[c, j], o_recv.at[c, j], at_z(down(j)))

    def y_copy(c):
        return remote(ysend.at[span(c, BLK), :], yrecv.at[span(c, BLK), :], y_send.at[c], y_recv.at[c], y_peer)

    def own_kv(a):
        return pltpu.make_async_copy(pairs[a][0].at[:, span(z, wide)], pairs[a][1].at[frame(z, x), :], own_sem.at[a])

    def own_query(c):
        return pltpu.make_async_copy(q_ref.at[span(c, BLK), span(z, wide)], qbuf.at[span(c * nz + z, BLK), :], own_q.at[c])

    def own_out(c):
        return pltpu.make_async_copy(obuf.at[span(c * nz + z, BLK), :], oin.at[span(c, BLK), span(z, wide)], own_o.at[c])

    def out_copy(c):
        return pltpu.make_async_copy(mine.at[span(c, BLK), :], out_ref.at[span(c, BLK), :], out_sem.at[c])

    for a in range(2):
        for j in range(nz - 1, 0, -1):
            kv_copy(a, j).start()
        x_copy(a, 0).start()
        own_kv(a).start()
    for c in range(blocks):
        own_query(c).start()

    key_block = lax.broadcasted_iota(jnp.int32, (1, bias.shape[1]), 1) // BLK

    @pl.loop(0, blocks * nz)
    def make_bias(i):
        c, zz = i // nz, lax.rem(i, nz)
        b = (zz * 2 + x) * blocks + c
        used = count_ref[b]
        line = jnp.full((1, bias.shape[1]), -1e30, jnp.float32)
        for s in range(slots):
            listed = jnp.where(s < used, list_ref[b, s], -1)
            line = jnp.where(key_block == listed, 0.0, line)
        bias[pl.ds(i, 1), :] = line

    def attend(query, key, value, lines):
        score = lax.dot_general(query, key, (((1,), (1,)), ((), ())), preferred_element_type=jnp.float32)
        if lines is not None:
            score = jnp.concatenate(
                [score[i * BLK:(i + 1) * BLK] + line for i, line in enumerate(lines)], axis=0)
        top = jnp.max(score, axis=1, keepdims=True)
        weight = jnp.exp2((score - top) * factor)
        total = jnp.sum(weight, axis=1, keepdims=True)
        summed = jnp.dot(weight.astype(jnp.bfloat16), value, preferred_element_type=jnp.float32)
        return (summed / total).astype(jnp.bfloat16)

    @pl.loop(0, nz)
    def cross(g):
        cols = span(g, wide)
        parts = [pltpu.make_async_copy(src.at[:, cols], dst, c_sem.at[n])
                 for n, (src, dst) in enumerate(((cq_ref, cqb), (tk_ref, tkb), (tv_ref, tvb)))]
        for part in parts:
            part.start()
        for part in parts:
            part.wait()

        @pl.loop(0, group)
        def one(h):
            head = span(h, DH)
            cob[:, head] = attend(cqb[:, head], tkb[:, head], tvb[:, head], None)

        back = pltpu.make_async_copy(cob, cross_ref.at[:, cols], c_sem.at[3])
        back.start()
        back.wait()

    for j in range(1, nz):
        kv_landing(0, j).wait_recv()
        x_copy(0, j).start()
    for c in range(blocks):
        for j in range(nz - 1, 0, -1):
            q_copy(c, j).start()
    for j in range(1, nz):
        kv_landing(1, j).wait_recv()
        x_copy(1, j).start()
    for a in range(2):
        own_kv(a).wait()
        for j in range(nz):
            x_landing(a, j).wait_recv()
    own_w.wait()

    tile = 512

    def project(c):
        own_out(c).wait()
        for j in range(1, nz):
            o_landing(c, j).wait_recv()
        here = span(c, BLK)

        def part(base, into):
            @pl.loop(0, half // tile)
            def columns(n):
                cols = pl.ds(pl.multiple_of(base * half + n * tile, tile), tile)
                into[here, span(n, tile)] = jnp.dot(
                    oin[here, :], wbuf[:, cols], preferred_element_type=jnp.float32).astype(jnp.bfloat16)

        part(1 - y, ysend)
        y_copy(c).start()
        part(y, mine)

    def finish(c):
        y_copy(c).wait_recv()
        here = span(c, BLK)
        mine[here, :] = (mine[here, :].astype(jnp.float32) + yrecv[here, :].astype(jnp.float32)).astype(jnp.bfloat16)
        out_copy(c).start()

    @pl.loop(0, blocks)
    def chunks(c):
        own_query(c).wait()
        for j in range(1, nz):
            q_landing(c, j).wait_recv()

        @pl.loop(0, group)
        def one(h):
            head = span(h, DH)
            for r in range(nz // 2):
                lines = [bias[pl.ds(c * nz + 2 * r + i, 1), :] for i in range(2)]
                here = span(c * (nz // 2) + r, 2 * BLK)
                obuf[here, head] = attend(qbuf[here, head], kbuf[:, head], vbuf[:, head], lines)

        for j in range(nz - 1, 0, -1):
            o_copy(c, j).start()
        own_out(c).start()

        @pl.when(c >= 1)
        def earlier():
            project(c - 1)

    project(blocks - 1)
    for c in range(blocks):
        finish(c)
    for c in range(blocks):
        out_copy(c).wait()
        y_copy(c).wait_send()
        for j in range(1, nz):
            q_copy(c, j).wait_send()
            o_copy(c, j).wait_send()
    for a in range(2):
        for j in range(nz):
            x_copy(a, j).wait_send()
        for j in range(1, nz):
            kv_copy(a, j).wait_send()


def fused(nseq, queries, keys, values, cross_query, text_keys, text_values, out_weight, block_list, block_count):
    nz = nseq // 2
    rows, width = queries.shape
    heads_here = width // DH
    group = heads_here // nz
    wide = group * DH
    blocks = rows // BLK
    tokens = nseq * rows
    text = text_keys.shape[0]
    half = out_weight.shape[1] // 2
    bf = jnp.bfloat16
    dma = pltpu.SemaphoreType.DMA
    hbm = pl.BlockSpec(memory_space=pl.ANY)
    smem = pl.BlockSpec(memory_space=pltpu.SMEM)
    return pl.pallas_call(
        functools.partial(fused_kernel, (nz, rows, group, text, block_list.shape[1])),
        out_shape=(jax.ShapeDtypeStruct((rows, half), bf), jax.ShapeDtypeStruct((rows, width), bf)),
        in_specs=[hbm] * 7 + [smem] * 2,
        out_specs=(hbm, hbm),
        scratch_shapes=[
            pltpu.VMEM((tokens, wide), bf), pltpu.VMEM((tokens, wide), bf),
            pltpu.VMEM((nz * rows, wide), bf), pltpu.VMEM((nz * rows, wide), bf),
            pltpu.VMEM((rows, width), bf), pltpu.VMEM(out_weight.shape, bf),
            pltpu.VMEM((rows, half), bf), pltpu.VMEM((rows, half), bf), pltpu.VMEM((rows, half), bf),
            pltpu.VMEM((nz * blocks, tokens), jnp.float32),
            pltpu.VMEM((rows, wide), bf), pltpu.VMEM((text, wide), bf), pltpu.VMEM((text, wide), bf),
            pltpu.VMEM((rows, wide), bf),
            dma((2, nz)), dma((2, nz)), dma((2, nz)), dma((2, nz)),
            dma((blocks, nz)), dma((blocks, nz)), dma((blocks, nz)), dma((blocks, nz)),
            dma((blocks,)), dma((blocks,)), dma((3,)), dma((blocks,)), dma((blocks,)), dma((4,)), dma((blocks,)),
        ],
        compiler_params=pltpu.CompilerParams(
            collective_id=0, has_side_effects=True, vmem_limit_bytes=62 * 1024 * 1024),
        cost_estimate=pl.CostEstimate(
            flops=4 * rows * tokens * width + 4 * rows * width * half + 4 * rows * text * width,
            bytes_accessed=2 * (6 * rows * width + 2 * text * width + 2 * width * half),
            transcendentals=rows * heads_here * (tokens + text)),
    )(queries, keys, values, cross_query, text_keys, text_values, out_weight, block_list, block_count)


def solution(mesh):
    in_specs = (
        P(("pair", "seq"), "head"),
        P(("pair", "seq"), "head"),
        P(("pair", "seq"), "head"),
        P(("pair", "seq"), "head"),
        P("pair", "head"),
        P("pair", "head"),
        P("head", None),
        P(),
        P(),
    )
    out_specs = (P(("pair", "seq"), "head"), P(("pair", "seq"), "head"))
    nseq = mesh.shape["seq"]

    def choose(*args):
        width = args[0].shape[1]
        nz = nseq // 2
        fits = mesh.shape["head"] == 2 and nseq % 4 == 0 and (width // DH) % nz == 0
        return functools.partial(fused, nseq)(*args) if fits else body(*args)

    return jax.shard_map(choose, mesh=mesh, in_specs=in_specs, out_specs=out_specs, check_vma=False)
```

```python
import functools

import jax
import jax.numpy as jnp
from jax import lax
from jax.experimental import pallas as pl
from jax.experimental.pallas import tpu as pltpu
from jax.sharding import PartitionSpec as P

DH = 128
BLK = 128


def allowed_table(block_list, block_count):
    slots = jnp.arange(block_list.shape[1], dtype=jnp.int32)
    targets = jnp.arange(block_list.shape[0], dtype=jnp.int32)
    hit = (block_list[:, :, None] == targets[None, None, :]) & (
        slots[None, :, None] < block_count[:, None, None]
    )
    return jnp.any(hit, axis=1).astype(jnp.int32)


def attend_tile(carry, query_three, key_tile, value_tile, tile_mask, scale):
    row_max, total, summed = carry
    count = key_tile.shape[0]
    heads_here = query_three.shape[1]
    key_three = key_tile.reshape(count, heads_here, DH)
    value_three = value_tile.reshape(count, heads_here, DH)
    score = (
        jnp.einsum("qhd,khd->hqk", query_three, key_three, preferred_element_type=jnp.float32)
        * scale
    )
    score = jnp.where(tile_mask[None], score, -1e30)
    new_max = jnp.maximum(row_max, jnp.max(score, axis=2))
    weight = jnp.where(tile_mask[None], jnp.exp(score - new_max[:, :, None]), 0.0)
    factor = jnp.exp(row_max - new_max)
    total = total * factor + jnp.sum(weight, axis=2)
    update = jnp.einsum(
        "hqk,khd->hqd", weight.astype(jnp.bfloat16), value_three, preferred_element_type=jnp.float32
    )
    summed = summed * factor[:, :, None] + update
    return (new_max, total, summed)


def masked_update(carry, query_three, key_tile, value_tile, tile_mask, scale):
    return attend_tile(carry, query_three, key_tile, value_tile, tile_mask, scale)


def empty_state(heads_here, count):
    return (
        jnp.full((heads_here, count), -1e30, jnp.float32),
        jnp.zeros((heads_here, count), jnp.float32),
        jnp.zeros((heads_here, count, DH), jnp.float32),
    )


def body(
    queries, keys, values, cross_query, text_keys, text_values, out_weight, block_list, block_count
):
    scale = DH ** (-0.5)
    rows = queries.shape[0]
    heads_here = queries.shape[1] // DH
    blocks_here = rows // BLK
    allowed = allowed_table(block_list, block_count) > 0
    my_first = lax.axis_index("seq") * blocks_here
    query_three = queries.reshape(rows, heads_here, DH)
    row_allowed = jnp.repeat(
        lax.dynamic_slice_in_dim(allowed, my_first, blocks_here, 0), BLK, axis=0
    )
    key_piece = lax.all_gather(keys, "seq", axis=0, tiled=True)
    value_piece = lax.all_gather(values, "seq", axis=0, tiled=True)
    count = key_piece.shape[0]
    shards_in = count // rows
    factor = 1
    for candidate in range(1, shards_in + 1):
        if shards_in % candidate == 0 and candidate * rows <= 1536:
            factor = candidate
    width = factor * rows
    piece_mask = jnp.repeat(row_allowed, BLK, axis=1)
    tiles = count // width
    key_tiles = key_piece.reshape(tiles, width, key_piece.shape[1])
    value_tiles = value_piece.reshape(tiles, width, value_piece.shape[1])
    mask_tiles = piece_mask.reshape(rows, tiles, width).transpose(1, 0, 2)

    def step(state, items):
        return (masked_update(state, query_three, items[0], items[1], items[2], scale), None)

    state, unused = lax.scan(
        step, empty_state(heads_here, rows), (key_tiles, value_tiles, mask_tiles)
    )
    row_max, total, summed = state
    self_three = (summed / total[:, :, None]).transpose(1, 0, 2)
    self_heads = self_three.reshape(rows, heads_here * DH).astype(jnp.bfloat16)
    term = jnp.dot(self_heads, out_weight, preferred_element_type=jnp.float32)
    block_stream = lax.psum_scatter(
        term.astype(jnp.bfloat16), "head", scatter_dimension=1, tiled=True
    )
    cross_three = cross_query.reshape(rows, heads_here, DH)
    text_count = text_keys.shape[0]
    text_key_three = text_keys.reshape(text_count, heads_here, DH)
    text_value_three = text_values.reshape(text_count, heads_here, DH)
    cross_score = (
        jnp.einsum("qhd,khd->hqk", cross_three, text_key_three, preferred_element_type=jnp.float32)
        * scale
    )
    cross_max = jnp.max(cross_score, axis=2, keepdims=True)
    cross_weight = jnp.exp(cross_score - cross_max)
    cross_total = jnp.sum(cross_weight, axis=2)
    cross_sum = jnp.einsum(
        "hqk,khd->hqd",
        cross_weight.astype(jnp.bfloat16),
        text_value_three,
        preferred_element_type=jnp.float32,
    )
    cross_heads = (
        (cross_sum / cross_total[:, :, None])
        .transpose(1, 0, 2)
        .reshape(rows, heads_here * DH)
        .astype(jnp.bfloat16)
    )
    return (block_stream, cross_heads)


def fused_kernel(
    sizes,
    q_ref, k_ref, v_ref, cq_ref, tk_ref, tv_ref, w_ref, list_ref, count_ref,
    out_ref, cross_ref,
    kbuf, vbuf, qbuf, obuf, oin, wbuf, mine, ysend, yrecv, bias, cqb, tkb, tvb, cob,
    kv_send, kv_recv, x_send, x_recv, q_send, q_recv, o_send, o_recv, y_send, y_recv, own_sem, own_q, own_o, c_sem, out_sem,
):
    nz, rows, group, text, slots = sizes
    wide = group * DH
    blocks = rows // BLK
    chunk = nz * BLK
    half = out_ref.shape[1]
    seq = lax.axis_index("seq")
    z, x = seq // 2, lax.rem(seq, 2)
    y = lax.axis_index("head")
    tile = 512
    factor = (DH ** (-0.5)) * 1.4426950408889634

    def at_z(zz):
        return {"seq": zz * 2 + x}

    def up(j):
        return lax.rem(z + j, nz)

    def down(j):
        return lax.rem(z + nz - j, nz)

    x_peer = {"seq": z * 2 + 1 - x}
    y_peer = {"head": 1 - y}

    def span(i, size):
        return pl.ds(pl.multiple_of(i * size, size), size)

    def remote(src, dst, send, recv, where):
        return pltpu.make_async_remote_copy(
            src_ref=src, dst_ref=dst, send_sem=send, recv_sem=recv,
            device_id=where, device_id_type=pl.DeviceIdType.MESH,
        )

    def frame(zz, xx):
        return span(zz * 2 + xx, rows)

    own_w = pltpu.make_async_copy(w_ref, wbuf, own_sem.at[2])
    own_w.start()

    barrier = pltpu.get_barrier_semaphore()
    for j in range(1, nz):
        pl.semaphore_signal(barrier, inc=1, device_id=at_z(up(j)), device_id_type=pl.DeviceIdType.MESH)
    pl.semaphore_signal(barrier, inc=1, device_id=x_peer, device_id_type=pl.DeviceIdType.MESH)
    pl.semaphore_signal(barrier, inc=1, device_id=y_peer, device_id_type=pl.DeviceIdType.MESH)
    pl.semaphore_wait(barrier, nz + 1)

    pairs = ((k_ref, kbuf), (v_ref, vbuf))
    early = blocks - 1

    def kv_copy(a, h, j):
        return remote(pairs[a][0].at[:, span(up(j) * group + h, DH)], pairs[a][1].at[frame(z, x), span(h, DH)],
                      kv_send.at[a * group + h, j], kv_recv.at[a * group + h, j], at_z(up(j)))

    def kv_landing(a, h, j):
        place = pairs[a][1].at[frame(down(j), x), span(h, DH)]
        return remote(place, place, kv_send.at[a * group + h, j], kv_recv.at[a * group + h, j], at_z(down(j)))

    def x_copy(a, h, j):
        place = pairs[a][1].at[frame(down(j), x), span(h, DH)]
        source = place if j else pairs[a][0].at[:, span(z * group + h, DH)]
        return remote(source, place, x_send.at[a * group + h, j], x_recv.at[a * group + h, j], x_peer)

    def x_landing(a, h, j):
        place = pairs[a][1].at[frame(down(j), 1 - x), span(h, DH)]
        return remote(place, place, x_send.at[a * group + h, j], x_recv.at[a * group + h, j], x_peer)

    def q_copy(c, j):
        return remote(q_ref.at[span(c, BLK), span(up(j), wide)], qbuf.at[span(c * nz + z, BLK), :],
                      q_send.at[c, j], q_recv.at[c, j], at_z(up(j)))

    def q_landing(c, j):
        place = qbuf.at[span(c * nz + down(j), BLK), :]
        return remote(place, place, q_send.at[c, j], q_recv.at[c, j], at_z(down(j)))

    def o_copy(c, h, j):
        return remote(obuf.at[span(c * nz + up(j), BLK), span(h, DH)], oin.at[span(c, BLK), span(z * group + h, DH)],
                      o_send.at[c * group + h, j], o_recv.at[c * group + h, j], at_z(up(j)))

    def o_landing(c, h, j):
        place = oin.at[span(c, BLK), span(down(j) * group + h, DH)]
        return remote(place, place, o_send.at[c * group + h, j], o_recv.at[c * group + h, j], at_z(down(j)))

    def y_copy(c, n):
        return remote(ysend.at[span(c, BLK), span(n, tile)], yrecv.at[span(c, BLK), span(n, tile)],
                      y_send.at[c, n], y_recv.at[c, n], y_peer)

    def own_kv(a):
        return pltpu.make_async_copy(pairs[a][0].at[:, span(z, wide)], pairs[a][1].at[frame(z, x), :], own_sem.at[a])

    def own_query(c):
        return pltpu.make_async_copy(q_ref.at[span(c, BLK), span(z, wide)], qbuf.at[span(c * nz + z, BLK), :], own_q.at[c])

    def own_out(c):
        return pltpu.make_async_copy(obuf.at[span(c * nz + z, BLK), :], oin.at[span(c, BLK), span(z, wide)], own_o.at[c])

    def out_copy(c):
        return pltpu.make_async_copy(mine.at[span(c, BLK), :], out_ref.at[span(c, BLK), :], out_sem.at[c])

    def send_queries(c):
        for j in range(nz - 1, 0, -1):
            q_copy(c, j).start()

    def send_head(h):
        for a in range(2):
            for j in range(nz - 1, 0, -1):
                kv_copy(a, h, j).start()
            x_copy(a, h, 0).start()

    send_queries(0)
    send_head(0)
    for c in range(1, early):
        send_queries(c)
    send_head(1)
    for a in range(2):
        own_kv(a).start()
    for c in range(blocks):
        own_query(c).start()

    key_block = lax.broadcasted_iota(jnp.int32, (1, bias.shape[1]), 1) // BLK

    @pl.loop(0, blocks * nz)
    def make_bias(i):
        c, zz = i // nz, lax.rem(i, nz)
        b = (zz * 2 + x) * blocks + c
        used = count_ref[b]
        line = jnp.full((1, bias.shape[1]), -1e30, jnp.float32)
        for s in range(slots):
            listed = jnp.where(s < used, list_ref[b, s], -1)
            line = jnp.where(key_block == listed, 0.0, line)
        bias[pl.ds(i, 1), :] = line

    def attend(query, key, value, lines):
        score = lax.dot_general(query, key, (((1,), (1,)), ((), ())), preferred_element_type=jnp.float32)
        if lines is not None:
            score = jnp.concatenate(
                [score[i * BLK:(i + 1) * BLK] + line for i, line in enumerate(lines)], axis=0)
        top = jnp.max(score, axis=1, keepdims=True)
        weight = jnp.exp2((score - top) * factor)
        total = jnp.sum(weight, axis=1, keepdims=True)
        summed = jnp.dot(weight.astype(jnp.bfloat16), value, preferred_element_type=jnp.float32)
        return (summed / total).astype(jnp.bfloat16)

    @pl.loop(0, nz)
    def cross(g):
        cols = span(g, wide)
        parts = [pltpu.make_async_copy(src.at[:, cols], dst, c_sem.at[n])
                 for n, (src, dst) in enumerate(((cq_ref, cqb), (tk_ref, tkb), (tv_ref, tvb)))]
        for part in parts:
            part.start()
        for part in parts:
            part.wait()

        @pl.loop(0, group)
        def one(h):
            head = span(h, DH)
            cob[:, head] = attend(cqb[:, head], tkb[:, head], tvb[:, head], None)

        back = pltpu.make_async_copy(cob, cross_ref.at[:, cols], c_sem.at[3])
        back.start()
        back.wait()

    def attend_chunk(c, h):
        head = span(h, DH)
        for r in range(nz // 2):
            lines = [bias[pl.ds(c * nz + 2 * r + i, 1), :] for i in range(2)]
            here = span(c * (nz // 2) + r, 2 * BLK)
            obuf[here, head] = attend(qbuf[here, head], kbuf[:, head], vbuf[:, head], lines)

    def wait_queries(c):
        own_query(c).wait()
        for j in range(1, nz):
            q_landing(c, j).wait_recv()

    def project(c):
        own_out(c).wait()

        @pl.loop(0, group)
        def arrived(h):
            for j in range(1, nz):
                o_landing(c, h, j).wait_recv()

        here = span(c, BLK)

        def product(base, n):
            cols = pl.ds(pl.multiple_of(base * half + n * tile, tile), tile)
            return jnp.dot(oin[here, :], wbuf[:, cols], preferred_element_type=jnp.float32).astype(jnp.bfloat16)

        @pl.loop(0, half // tile)
        def theirs(n):
            ysend[here, span(n, tile)] = product(1 - y, n)
            y_copy(c, n).start()

        @pl.loop(0, half // tile)
        def ours(n):
            mine[here, span(n, tile)] = product(y, n)

    def finish(c):
        here = span(c, BLK)

        @pl.loop(0, half // tile)
        def columns(n):
            y_copy(c, n).wait_recv()
            cols = span(n, tile)
            mine[here, cols] = (mine[here, cols].astype(jnp.float32) + yrecv[here, cols].astype(jnp.float32)).astype(jnp.bfloat16)

        out_copy(c).start()

    for a in range(2):
        own_kv(a).wait()

    @pl.loop(0, group + 1)
    def arrive(h):
        @pl.when(h < group)
        def pass_on():
            for a in range(2):
                for j in range(1, nz):
                    kv_landing(a, h, j).wait_recv()
                    x_copy(a, h, j).start()

        @pl.when(h + 2 < group)
        def more():
            send_head(h + 2)

        @pl.when(h == max(group - 2, 0))
        def last_queries():
            for c in range(early, blocks):
                send_queries(c)

        @pl.when(h == 1)
        def first_queries():
            for c in range(early):
                wait_queries(c)

        @pl.when(h >= 1)
        def compute():
            for a in range(2):
                for j in range(nz):
                    x_landing(a, h - 1, j).wait_recv()

            @pl.loop(0, early)
            def one(c):
                attend_chunk(c, h - 1)

    def send_outputs(c, h):
        for j in range(nz - 1, 0, -1):
            o_copy(c, h, j).start()

    @pl.loop(0, early)
    def give_back(c):
        own_out(c).start()

        @pl.loop(0, group)
        def one(h):
            send_outputs(c, h)

    own_w.wait()
    for c in range(early, blocks):
        wait_queries(c)

        @pl.loop(0, group)
        def one(h):
            attend_chunk(c, h)
            send_outputs(c, h)

        own_out(c).start()

    @pl.loop(0, blocks)
    def projected(c):
        project(c)

    @pl.loop(0, blocks)
    def finished(c):
        finish(c)

    @pl.loop(0, blocks)
    def drained(c):
        out_copy(c).wait()

        @pl.loop(0, half // tile)
        def one(n):
            y_copy(c, n).wait_send()

        @pl.loop(0, group)
        def two(h):
            for j in range(1, nz):
                o_copy(c, h, j).wait_send()

        for j in range(1, nz):
            q_copy(c, j).wait_send()

    @pl.loop(0, group)
    def heads_sent(h):
        for a in range(2):
            for j in range(nz):
                x_copy(a, h, j).wait_send()
            for j in range(1, nz):
                kv_copy(a, h, j).wait_send()


def fused(nseq, queries, keys, values, cross_query, text_keys, text_values, out_weight, block_list, block_count):
    nz = nseq // 2
    rows, width = queries.shape
    heads_here = width // DH
    group = heads_here // nz
    wide = group * DH
    blocks = rows // BLK
    tokens = nseq * rows
    text = text_keys.shape[0]
    half = out_weight.shape[1] // 2
    bf = jnp.bfloat16
    dma = pltpu.SemaphoreType.DMA
    hbm = pl.BlockSpec(memory_space=pl.ANY)
    smem = pl.BlockSpec(memory_space=pltpu.SMEM)
    return pl.pallas_call(
        functools.partial(fused_kernel, (nz, rows, group, text, block_list.shape[1])),
        out_shape=(jax.ShapeDtypeStruct((rows, half), bf), jax.ShapeDtypeStruct((rows, width), bf)),
        in_specs=[hbm] * 7 + [smem] * 2,
        out_specs=(hbm, hbm),
        scratch_shapes=[
            pltpu.VMEM((tokens, wide), bf), pltpu.VMEM((tokens, wide), bf),
            pltpu.VMEM((nz * rows, wide), bf), pltpu.VMEM((nz * rows, wide), bf),
            pltpu.VMEM((rows, width), bf), pltpu.VMEM(out_weight.shape, bf),
            pltpu.VMEM((rows, half), bf), pltpu.VMEM((rows, half), bf), pltpu.VMEM((rows, half), bf),
            pltpu.VMEM((nz * blocks, tokens), jnp.float32),
            pltpu.VMEM((rows, wide), bf), pltpu.VMEM((text, wide), bf), pltpu.VMEM((text, wide), bf),
            pltpu.VMEM((rows, wide), bf),
            dma((2 * group, nz)), dma((2 * group, nz)), dma((2 * group, nz)), dma((2 * group, nz)),
            dma((blocks, nz)), dma((blocks, nz)), dma((blocks * group, nz)), dma((blocks * group, nz)),
            dma((blocks, half // 512)), dma((blocks, half // 512)), dma((3,)), dma((blocks,)), dma((blocks,)), dma((4,)), dma((blocks,)),
        ],
        compiler_params=pltpu.CompilerParams(
            collective_id=0, has_side_effects=True, vmem_limit_bytes=62 * 1024 * 1024),
        cost_estimate=pl.CostEstimate(
            flops=4 * rows * tokens * width + 4 * rows * width * half + 4 * rows * text * width,
            bytes_accessed=2 * (6 * rows * width + 2 * text * width + 2 * width * half),
            transcendentals=rows * heads_here * (tokens + text)),
    )(queries, keys, values, cross_query, text_keys, text_values, out_weight, block_list, block_count)


def solution(mesh):
    in_specs = (
        P(("pair", "seq"), "head"),
        P(("pair", "seq"), "head"),
        P(("pair", "seq"), "head"),
        P(("pair", "seq"), "head"),
        P("pair", "head"),
        P("pair", "head"),
        P("head", None),
        P(),
        P(),
    )
    out_specs = (P(("pair", "seq"), "head"), P(("pair", "seq"), "head"))
    nseq = mesh.shape["seq"]

    def choose(*args):
        width = args[0].shape[1]
        nz = nseq // 2
        fits = mesh.shape["head"] == 2 and nseq % 4 == 0 and (width // DH) % nz == 0 and width // DH >= 2 * nz
        return functools.partial(fused, nseq)(*args) if fits else body(*args)

    return jax.shard_map(choose, mesh=mesh, in_specs=in_specs, out_specs=out_specs, check_vma=False)
```

```python
import functools

import jax
import jax.numpy as jnp
from jax import lax
from jax.experimental import pallas as pl
from jax.experimental.pallas import tpu as pltpu
from jax.sharding import PartitionSpec as P

DH = 128
BLK = 128


def allowed_table(block_list, block_count):
    slots = jnp.arange(block_list.shape[1], dtype=jnp.int32)
    targets = jnp.arange(block_list.shape[0], dtype=jnp.int32)
    hit = (block_list[:, :, None] == targets[None, None, :]) & (
        slots[None, :, None] < block_count[:, None, None]
    )
    return jnp.any(hit, axis=1).astype(jnp.int32)


def attend_tile(carry, query_three, key_tile, value_tile, tile_mask, scale):
    row_max, total, summed = carry
    count = key_tile.shape[0]
    heads_here = query_three.shape[1]
    key_three = key_tile.reshape(count, heads_here, DH)
    value_three = value_tile.reshape(count, heads_here, DH)
    score = (
        jnp.einsum("qhd,khd->hqk", query_three, key_three, preferred_element_type=jnp.float32)
        * scale
    )
    score = jnp.where(tile_mask[None], score, -1e30)
    new_max = jnp.maximum(row_max, jnp.max(score, axis=2))
    weight = jnp.where(tile_mask[None], jnp.exp(score - new_max[:, :, None]), 0.0)
    factor = jnp.exp(row_max - new_max)
    total = total * factor + jnp.sum(weight, axis=2)
    update = jnp.einsum(
        "hqk,khd->hqd", weight.astype(jnp.bfloat16), value_three, preferred_element_type=jnp.float32
    )
    summed = summed * factor[:, :, None] + update
    return (new_max, total, summed)


def masked_update(carry, query_three, key_tile, value_tile, tile_mask, scale):
    return attend_tile(carry, query_three, key_tile, value_tile, tile_mask, scale)


def empty_state(heads_here, count):
    return (
        jnp.full((heads_here, count), -1e30, jnp.float32),
        jnp.zeros((heads_here, count), jnp.float32),
        jnp.zeros((heads_here, count, DH), jnp.float32),
    )


def body(
    queries, keys, values, cross_query, text_keys, text_values, out_weight, block_list, block_count
):
    scale = DH ** (-0.5)
    rows = queries.shape[0]
    heads_here = queries.shape[1] // DH
    blocks_here = rows // BLK
    allowed = allowed_table(block_list, block_count) > 0
    my_first = lax.axis_index("seq") * blocks_here
    query_three = queries.reshape(rows, heads_here, DH)
    row_allowed = jnp.repeat(
        lax.dynamic_slice_in_dim(allowed, my_first, blocks_here, 0), BLK, axis=0
    )
    key_piece = lax.all_gather(keys, "seq", axis=0, tiled=True)
    value_piece = lax.all_gather(values, "seq", axis=0, tiled=True)
    count = key_piece.shape[0]
    shards_in = count // rows
    factor = 1
    for candidate in range(1, shards_in + 1):
        if shards_in % candidate == 0 and candidate * rows <= 1536:
            factor = candidate
    width = factor * rows
    piece_mask = jnp.repeat(row_allowed, BLK, axis=1)
    tiles = count // width
    key_tiles = key_piece.reshape(tiles, width, key_piece.shape[1])
    value_tiles = value_piece.reshape(tiles, width, value_piece.shape[1])
    mask_tiles = piece_mask.reshape(rows, tiles, width).transpose(1, 0, 2)

    def step(state, items):
        return (masked_update(state, query_three, items[0], items[1], items[2], scale), None)

    state, unused = lax.scan(
        step, empty_state(heads_here, rows), (key_tiles, value_tiles, mask_tiles)
    )
    row_max, total, summed = state
    self_three = (summed / total[:, :, None]).transpose(1, 0, 2)
    self_heads = self_three.reshape(rows, heads_here * DH).astype(jnp.bfloat16)
    term = jnp.dot(self_heads, out_weight, preferred_element_type=jnp.float32)
    block_stream = lax.psum_scatter(
        term.astype(jnp.bfloat16), "head", scatter_dimension=1, tiled=True
    )
    cross_three = cross_query.reshape(rows, heads_here, DH)
    text_count = text_keys.shape[0]
    text_key_three = text_keys.reshape(text_count, heads_here, DH)
    text_value_three = text_values.reshape(text_count, heads_here, DH)
    cross_score = (
        jnp.einsum("qhd,khd->hqk", cross_three, text_key_three, preferred_element_type=jnp.float32)
        * scale
    )
    cross_max = jnp.max(cross_score, axis=2, keepdims=True)
    cross_weight = jnp.exp(cross_score - cross_max)
    cross_total = jnp.sum(cross_weight, axis=2)
    cross_sum = jnp.einsum(
        "hqk,khd->hqd",
        cross_weight.astype(jnp.bfloat16),
        text_value_three,
        preferred_element_type=jnp.float32,
    )
    cross_heads = (
        (cross_sum / cross_total[:, :, None])
        .transpose(1, 0, 2)
        .reshape(rows, heads_here * DH)
        .astype(jnp.bfloat16)
    )
    return (block_stream, cross_heads)


def fused_kernel(
    sizes,
    q_ref, k_ref, v_ref, cq_ref, tk_ref, tv_ref, w_ref, list_ref, count_ref,
    out_ref, cross_ref,
    kbuf, vbuf, qbuf, obuf, oin, wbuf, mine, ysend, yrecv, bias, cqb, tkb, tvb, cob,
    kv_send, kv_recv, x_send, x_recv, q_send, q_recv, o_send, o_recv, y_send, y_recv, own_sem, own_q, own_o, c_sem, out_sem,
):
    nz, rows, group, text, slots = sizes
    wide = group * DH
    blocks = rows // BLK
    chunk = nz * BLK
    half = out_ref.shape[1]
    seq = lax.axis_index("seq")
    z, x = seq // 2, lax.rem(seq, 2)
    y = lax.axis_index("head")
    tile = 512
    factor = (DH ** (-0.5)) * 1.4426950408889634

    def at_z(zz):
        return {"seq": zz * 2 + x}

    def up(j):
        return lax.rem(z + j, nz)

    def down(j):
        return lax.rem(z + nz - j, nz)

    x_peer = {"seq": z * 2 + 1 - x}
    y_peer = {"head": 1 - y}

    def span(i, size):
        return pl.ds(pl.multiple_of(i * size, size), size)

    def remote(src, dst, send, recv, where):
        return pltpu.make_async_remote_copy(
            src_ref=src, dst_ref=dst, send_sem=send, recv_sem=recv,
            device_id=where, device_id_type=pl.DeviceIdType.MESH,
        )

    def frame(zz, xx):
        return span(zz * 2 + xx, rows)

    own_w = pltpu.make_async_copy(w_ref, wbuf, own_sem.at[2])
    own_w.start()

    barrier = pltpu.get_barrier_semaphore()
    for j in range(1, nz):
        pl.semaphore_signal(barrier, inc=1, device_id=at_z(up(j)), device_id_type=pl.DeviceIdType.MESH)
    pl.semaphore_signal(barrier, inc=1, device_id=x_peer, device_id_type=pl.DeviceIdType.MESH)
    pl.semaphore_signal(barrier, inc=1, device_id=y_peer, device_id_type=pl.DeviceIdType.MESH)
    pl.semaphore_wait(barrier, nz + 1)

    pairs = ((k_ref, kbuf), (v_ref, vbuf))
    early = blocks - 1

    def kv_copy(a, h, j):
        return remote(pairs[a][0].at[:, span(up(j) * group + h, DH)], pairs[a][1].at[frame(z, x), span(h, DH)],
                      kv_send.at[a * group + h, j], kv_recv.at[a * group + h, j], at_z(up(j)))

    def kv_landing(a, h, j):
        place = pairs[a][1].at[frame(down(j), x), span(h, DH)]
        return remote(place, place, kv_send.at[a * group + h, j], kv_recv.at[a * group + h, j], at_z(down(j)))

    def x_copy(a, h, j):
        place = pairs[a][1].at[frame(down(j), x), span(h, DH)]
        source = place if j else pairs[a][0].at[:, span(z * group + h, DH)]
        return remote(source, place, x_send.at[a * group + h, j], x_recv.at[a * group + h, j], x_peer)

    def x_landing(a, h, j):
        place = pairs[a][1].at[frame(down(j), 1 - x), span(h, DH)]
        return remote(place, place, x_send.at[a * group + h, j], x_recv.at[a * group + h, j], x_peer)

    def part_of(unit, zz):
        u, start, size = unit
        return pl.ds(pl.multiple_of(start * nz + zz * size, size), size)

    def rows_of(unit):
        u, start, size = unit
        return pl.ds(pl.multiple_of(start, size), size)

    def q_copy(unit, j):
        return remote(q_ref.at[rows_of(unit), span(up(j), wide)], qbuf.at[part_of(unit, z), :],
                      q_send.at[unit[0], j], q_recv.at[unit[0], j], at_z(up(j)))

    def q_landing(unit, j):
        place = qbuf.at[part_of(unit, down(j)), :]
        return remote(place, place, q_send.at[unit[0], j], q_recv.at[unit[0], j], at_z(down(j)))

    def o_copy(unit, h, j):
        mark = unit[0] * group + h
        return remote(obuf.at[part_of(unit, up(j)), span(h, DH)], oin.at[rows_of(unit), span(z * group + h, DH)],
                      o_send.at[mark, j], o_recv.at[mark, j], at_z(up(j)))

    def o_landing(unit, h, j):
        mark = unit[0] * group + h
        place = oin.at[rows_of(unit), span(down(j) * group + h, DH)]
        return remote(place, place, o_send.at[mark, j], o_recv.at[mark, j], at_z(down(j)))

    def y_copy(unit, n):
        here = rows_of(unit)
        return remote(ysend.at[here, span(n, tile)], yrecv.at[here, span(n, tile)],
                      y_send.at[unit[0], n], y_recv.at[unit[0], n], y_peer)

    def own_kv(a):
        return pltpu.make_async_copy(pairs[a][0].at[:, span(z, wide)], pairs[a][1].at[frame(z, x), :], own_sem.at[a])

    def own_query(unit):
        return pltpu.make_async_copy(q_ref.at[rows_of(unit), span(z, wide)], qbuf.at[part_of(unit, z), :], own_q.at[unit[0]])

    def own_out(unit):
        return pltpu.make_async_copy(obuf.at[part_of(unit, z), :], oin.at[rows_of(unit), span(z, wide)], own_o.at[unit[0]])

    def out_copy(unit):
        here = rows_of(unit)
        return pltpu.make_async_copy(mine.at[here, :], out_ref.at[here, :], out_sem.at[unit[0]])

    def early_unit(c):
        return (c, c * BLK, BLK)

    cut = BLK // 2
    late = [(early + i, early * BLK + i * cut, cut) for i in range(2)]
    units = [early_unit(c) for c in range(early)] + late

    def send_queries(unit):
        for j in range(nz - 1, 0, -1):
            q_copy(unit, j).start()

    def send_head(h):
        for a in range(2):
            for j in range(nz - 1, 0, -1):
                kv_copy(a, h, j).start()
            x_copy(a, h, 0).start()

    send_queries(units[0])
    send_head(0)
    for c in range(1, early):
        send_queries(units[c])
    send_head(1)
    for a in range(2):
        own_kv(a).start()
    for unit in units:
        own_query(unit).start()

    key_block = lax.broadcasted_iota(jnp.int32, (1, bias.shape[1]), 1) // BLK

    @pl.loop(0, blocks * nz)
    def make_bias(i):
        c, zz = i // nz, lax.rem(i, nz)
        b = (zz * 2 + x) * blocks + c
        used = count_ref[b]
        line = jnp.full((1, bias.shape[1]), -1e30, jnp.float32)
        for s in range(slots):
            listed = jnp.where(s < used, list_ref[b, s], -1)
            line = jnp.where(key_block == listed, 0.0, line)
        bias[pl.ds(i, 1), :] = line

    def attend(query, key, value, lines):
        score = lax.dot_general(query, key, (((1,), (1,)), ((), ())), preferred_element_type=jnp.float32)
        if lines is not None:
            step = score.shape[0] // len(lines)
            score = jnp.concatenate(
                [score[i * step:(i + 1) * step] + line for i, line in enumerate(lines)], axis=0)
        top = jnp.max(score, axis=1, keepdims=True)
        weight = jnp.exp2((score - top) * factor)
        total = jnp.sum(weight, axis=1, keepdims=True)
        summed = jnp.dot(weight.astype(jnp.bfloat16), value, preferred_element_type=jnp.float32)
        return (summed / total).astype(jnp.bfloat16)

    @pl.loop(0, nz)
    def cross(g):
        cols = span(g, wide)
        parts = [pltpu.make_async_copy(src.at[:, cols], dst, c_sem.at[n])
                 for n, (src, dst) in enumerate(((cq_ref, cqb), (tk_ref, tkb), (tv_ref, tvb)))]
        for part in parts:
            part.start()
        for part in parts:
            part.wait()

        @pl.loop(0, group)
        def one(h):
            head = span(h, DH)
            cob[:, head] = attend(cqb[:, head], tkb[:, head], tvb[:, head], None)

        back = pltpu.make_async_copy(cob, cross_ref.at[:, cols], c_sem.at[3])
        back.start()
        back.wait()

    def attend_chunk(unit, block, h):
        u, start, size = unit
        head = span(h, DH)
        many = 2 * BLK // size
        for r in range(nz // many):
            lines = [bias[pl.ds(block * nz + many * r + i, 1), :] for i in range(many)]
            here = pl.ds(pl.multiple_of(start * nz + r * 2 * BLK, 2 * BLK), 2 * BLK)
            obuf[here, head] = attend(qbuf[here, head], kbuf[:, head], vbuf[:, head], lines)

    def wait_queries(unit):
        own_query(unit).wait()
        for j in range(1, nz):
            q_landing(unit, j).wait_recv()

    def project(unit):
        own_out(unit).wait()

        @pl.loop(0, group)
        def arrived(h):
            for j in range(1, nz):
                o_landing(unit, h, j).wait_recv()

        here = rows_of(unit)

        def product(base, n):
            cols = pl.ds(pl.multiple_of(base * half + n * tile, tile), tile)
            return jnp.dot(oin[here, :], wbuf[:, cols], preferred_element_type=jnp.float32).astype(jnp.bfloat16)

        @pl.loop(0, half // tile)
        def theirs(n):
            ysend[here, span(n, tile)] = product(1 - y, n)
            y_copy(unit, n).start()

        @pl.loop(0, half // tile)
        def ours(n):
            mine[here, span(n, tile)] = product(y, n)

    def finish(unit):
        here = rows_of(unit)

        @pl.loop(0, half // tile)
        def columns(n):
            y_copy(unit, n).wait_recv()
            cols = span(n, tile)
            mine[here, cols] = (mine[here, cols].astype(jnp.float32) + yrecv[here, cols].astype(jnp.float32)).astype(jnp.bfloat16)

        out_copy(unit).start()

    for a in range(2):
        own_kv(a).wait()

    @pl.loop(0, group + 1)
    def arrive(h):
        @pl.when(h < group)
        def pass_on():
            for a in range(2):
                for j in range(1, nz):
                    kv_landing(a, h, j).wait_recv()
                    x_copy(a, h, j).start()

        @pl.when(h + 2 < group)
        def more():
            send_head(h + 2)

        @pl.when(h == max(group - 2, 0))
        def last_queries():
            for unit in late:
                send_queries(unit)

        @pl.when(h == 1)
        def first_queries():
            for c in range(early):
                wait_queries(units[c])

        @pl.when(h >= 1)
        def compute():
            for a in range(2):
                for j in range(nz):
                    x_landing(a, h - 1, j).wait_recv()

            @pl.loop(0, early)
            def one(c):
                attend_chunk(early_unit(c), c, h - 1)

    def send_outputs(unit, h):
        for j in range(nz - 1, 0, -1):
            o_copy(unit, h, j).start()

    @pl.loop(0, early)
    def give_back(c):
        own_out(early_unit(c)).start()

        @pl.loop(0, group)
        def one(h):
            send_outputs(early_unit(c), h)

    own_w.wait()
    for i, unit in enumerate(late):
        wait_queries(unit)

        @pl.loop(0, group)
        def one(h):
            attend_chunk(unit, early, h)
            send_outputs(unit, h)

        own_out(unit).start()
        if i == 0:
            project(units[0])

    @pl.loop(1, early)
    def projected(c):
        project(early_unit(c))

    for unit in late:
        project(unit)

    for unit in units:
        finish(unit)

    for unit in units:
        out_copy(unit).wait()

        @pl.loop(0, half // tile)
        def one(n):
            y_copy(unit, n).wait_send()

        @pl.loop(0, group)
        def two(h):
            for j in range(1, nz):
                o_copy(unit, h, j).wait_send()

        for j in range(1, nz):
            q_copy(unit, j).wait_send()

    @pl.loop(0, group)
    def heads_sent(h):
        for a in range(2):
            for j in range(nz):
                x_copy(a, h, j).wait_send()
            for j in range(1, nz):
                kv_copy(a, h, j).wait_send()


def fused(nseq, queries, keys, values, cross_query, text_keys, text_values, out_weight, block_list, block_count):
    nz = nseq // 2
    rows, width = queries.shape
    heads_here = width // DH
    group = heads_here // nz
    wide = group * DH
    blocks = rows // BLK
    units = blocks + 1
    tokens = nseq * rows
    text = text_keys.shape[0]
    half = out_weight.shape[1] // 2
    bf = jnp.bfloat16
    dma = pltpu.SemaphoreType.DMA
    hbm = pl.BlockSpec(memory_space=pl.ANY)
    smem = pl.BlockSpec(memory_space=pltpu.SMEM)
    return pl.pallas_call(
        functools.partial(fused_kernel, (nz, rows, group, text, block_list.shape[1])),
        out_shape=(jax.ShapeDtypeStruct((rows, half), bf), jax.ShapeDtypeStruct((rows, width), bf)),
        in_specs=[hbm] * 7 + [smem] * 2,
        out_specs=(hbm, hbm),
        scratch_shapes=[
            pltpu.VMEM((tokens, wide), bf), pltpu.VMEM((tokens, wide), bf),
            pltpu.VMEM((nz * rows, wide), bf), pltpu.VMEM((nz * rows, wide), bf),
            pltpu.VMEM((rows, width), bf), pltpu.VMEM(out_weight.shape, bf),
            pltpu.VMEM((rows, half), bf), pltpu.VMEM((rows, half), bf), pltpu.VMEM((rows, half), bf),
            pltpu.VMEM((nz * blocks, tokens), jnp.float32),
            pltpu.VMEM((rows, wide), bf), pltpu.VMEM((text, wide), bf), pltpu.VMEM((text, wide), bf),
            pltpu.VMEM((rows, wide), bf),
            dma((2 * group, nz)), dma((2 * group, nz)), dma((2 * group, nz)), dma((2 * group, nz)),
            dma((units, nz)), dma((units, nz)), dma((units * group, nz)), dma((units * group, nz)),
            dma((units, half // 512)), dma((units, half // 512)), dma((3,)), dma((units,)), dma((units,)), dma((4,)), dma((units,)),
        ],
        compiler_params=pltpu.CompilerParams(
            collective_id=0, has_side_effects=True, vmem_limit_bytes=62 * 1024 * 1024),
        cost_estimate=pl.CostEstimate(
            flops=4 * rows * tokens * width + 4 * rows * width * half + 4 * rows * text * width,
            bytes_accessed=2 * (6 * rows * width + 2 * text * width + 2 * width * half),
            transcendentals=rows * heads_here * (tokens + text)),
    )(queries, keys, values, cross_query, text_keys, text_values, out_weight, block_list, block_count)


def solution(mesh):
    in_specs = (
        P(("pair", "seq"), "head"),
        P(("pair", "seq"), "head"),
        P(("pair", "seq"), "head"),
        P(("pair", "seq"), "head"),
        P("pair", "head"),
        P("pair", "head"),
        P("head", None),
        P(),
        P(),
    )
    out_specs = (P(("pair", "seq"), "head"), P(("pair", "seq"), "head"))
    nseq = mesh.shape["seq"]

    def choose(*args):
        width = args[0].shape[1]
        nz = nseq // 2
        fits = mesh.shape["head"] == 2 and nseq % 4 == 0 and (width // DH) % nz == 0 and width // DH >= 2 * nz
        return functools.partial(fused, nseq)(*args) if fits else body(*args)

    return jax.shard_map(choose, mesh=mesh, in_specs=in_specs, out_specs=out_specs, check_vma=False)
```

```python
import functools

import jax
import jax.numpy as jnp
from jax import lax
from jax.experimental import pallas as pl
from jax.experimental.pallas import tpu as pltpu
from jax.sharding import PartitionSpec as P

DH = 128
BLK = 128


def allowed_table(block_list, block_count):
    slots = jnp.arange(block_list.shape[1], dtype=jnp.int32)
    targets = jnp.arange(block_list.shape[0], dtype=jnp.int32)
    hit = (block_list[:, :, None] == targets[None, None, :]) & (
        slots[None, :, None] < block_count[:, None, None]
    )
    return jnp.any(hit, axis=1).astype(jnp.int32)


def attend_tile(carry, query_three, key_tile, value_tile, tile_mask, scale):
    row_max, total, summed = carry
    count = key_tile.shape[0]
    heads_here = query_three.shape[1]
    key_three = key_tile.reshape(count, heads_here, DH)
    value_three = value_tile.reshape(count, heads_here, DH)
    score = (
        jnp.einsum("qhd,khd->hqk", query_three, key_three, preferred_element_type=jnp.float32)
        * scale
    )
    score = jnp.where(tile_mask[None], score, -1e30)
    new_max = jnp.maximum(row_max, jnp.max(score, axis=2))
    weight = jnp.where(tile_mask[None], jnp.exp(score - new_max[:, :, None]), 0.0)
    factor = jnp.exp(row_max - new_max)
    total = total * factor + jnp.sum(weight, axis=2)
    update = jnp.einsum(
        "hqk,khd->hqd", weight.astype(jnp.bfloat16), value_three, preferred_element_type=jnp.float32
    )
    summed = summed * factor[:, :, None] + update
    return (new_max, total, summed)


def masked_update(carry, query_three, key_tile, value_tile, tile_mask, scale):
    return attend_tile(carry, query_three, key_tile, value_tile, tile_mask, scale)


def empty_state(heads_here, count):
    return (
        jnp.full((heads_here, count), -1e30, jnp.float32),
        jnp.zeros((heads_here, count), jnp.float32),
        jnp.zeros((heads_here, count, DH), jnp.float32),
    )


def body(
    queries, keys, values, cross_query, text_keys, text_values, out_weight, block_list, block_count
):
    scale = DH ** (-0.5)
    rows = queries.shape[0]
    heads_here = queries.shape[1] // DH
    blocks_here = rows // BLK
    allowed = allowed_table(block_list, block_count) > 0
    my_first = lax.axis_index("seq") * blocks_here
    query_three = queries.reshape(rows, heads_here, DH)
    row_allowed = jnp.repeat(
        lax.dynamic_slice_in_dim(allowed, my_first, blocks_here, 0), BLK, axis=0
    )
    key_piece = lax.all_gather(keys, "seq", axis=0, tiled=True)
    value_piece = lax.all_gather(values, "seq", axis=0, tiled=True)
    count = key_piece.shape[0]
    shards_in = count // rows
    factor = 1
    for candidate in range(1, shards_in + 1):
        if shards_in % candidate == 0 and candidate * rows <= 1536:
            factor = candidate
    width = factor * rows
    piece_mask = jnp.repeat(row_allowed, BLK, axis=1)
    tiles = count // width
    key_tiles = key_piece.reshape(tiles, width, key_piece.shape[1])
    value_tiles = value_piece.reshape(tiles, width, value_piece.shape[1])
    mask_tiles = piece_mask.reshape(rows, tiles, width).transpose(1, 0, 2)

    def step(state, items):
        return (masked_update(state, query_three, items[0], items[1], items[2], scale), None)

    state, unused = lax.scan(
        step, empty_state(heads_here, rows), (key_tiles, value_tiles, mask_tiles)
    )
    row_max, total, summed = state
    self_three = (summed / total[:, :, None]).transpose(1, 0, 2)
    self_heads = self_three.reshape(rows, heads_here * DH).astype(jnp.bfloat16)
    term = jnp.dot(self_heads, out_weight, preferred_element_type=jnp.float32)
    block_stream = lax.psum_scatter(
        term.astype(jnp.bfloat16), "head", scatter_dimension=1, tiled=True
    )
    cross_three = cross_query.reshape(rows, heads_here, DH)
    text_count = text_keys.shape[0]
    text_key_three = text_keys.reshape(text_count, heads_here, DH)
    text_value_three = text_values.reshape(text_count, heads_here, DH)
    cross_score = (
        jnp.einsum("qhd,khd->hqk", cross_three, text_key_three, preferred_element_type=jnp.float32)
        * scale
    )
    cross_max = jnp.max(cross_score, axis=2, keepdims=True)
    cross_weight = jnp.exp(cross_score - cross_max)
    cross_total = jnp.sum(cross_weight, axis=2)
    cross_sum = jnp.einsum(
        "hqk,khd->hqd",
        cross_weight.astype(jnp.bfloat16),
        text_value_three,
        preferred_element_type=jnp.float32,
    )
    cross_heads = (
        (cross_sum / cross_total[:, :, None])
        .transpose(1, 0, 2)
        .reshape(rows, heads_here * DH)
        .astype(jnp.bfloat16)
    )
    return (block_stream, cross_heads)


def fused_kernel(
    sizes,
    q_ref, k_ref, v_ref, cq_ref, tk_ref, tv_ref, w_ref, list_ref, count_ref,
    out_ref, cross_ref,
    kbuf, vbuf, qbuf, obuf, oin, wbuf, mine, ysend, yrecv, bias, cqb, tkb, tvb, cob,
    kv_send, kv_recv, x_send, x_recv, q_send, q_recv, o_send, o_recv, y_send, y_recv, own_sem, own_q, own_o, c_sem, out_sem,
):
    nz, rows, group, text, slots = sizes
    wide = group * DH
    blocks = rows // BLK
    chunk = nz * BLK
    half = out_ref.shape[1]
    seq = lax.axis_index("seq")
    z, x = seq // 2, lax.rem(seq, 2)
    y = lax.axis_index("head")
    tile = 512
    factor = (DH ** (-0.5)) * 1.4426950408889634

    def at_z(zz):
        return {"seq": zz * 2 + x}

    def up(j):
        return lax.rem(z + j, nz)

    def down(j):
        return lax.rem(z + nz - j, nz)

    x_peer = {"seq": z * 2 + 1 - x}
    y_peer = {"head": 1 - y}

    def span(i, size):
        return pl.ds(pl.multiple_of(i * size, size), size)

    def remote(src, dst, send, recv, where):
        return pltpu.make_async_remote_copy(
            src_ref=src, dst_ref=dst, send_sem=send, recv_sem=recv,
            device_id=where, device_id_type=pl.DeviceIdType.MESH,
        )

    def frame(zz, xx):
        return span(zz * 2 + xx, rows)

    own_w = pltpu.make_async_copy(w_ref, wbuf, own_sem.at[2])
    own_w.start()

    barrier = pltpu.get_barrier_semaphore()
    for j in range(1, nz):
        pl.semaphore_signal(barrier, inc=1, device_id=at_z(up(j)), device_id_type=pl.DeviceIdType.MESH)
    pl.semaphore_signal(barrier, inc=1, device_id=x_peer, device_id_type=pl.DeviceIdType.MESH)
    pl.semaphore_signal(barrier, inc=1, device_id=y_peer, device_id_type=pl.DeviceIdType.MESH)
    pl.semaphore_wait(barrier, nz + 1)

    pairs = ((k_ref, kbuf), (v_ref, vbuf))
    early = blocks - 1

    def kv_copy(a, h, j):
        return remote(pairs[a][0].at[:, span(up(j) * group + h, DH)], pairs[a][1].at[frame(z, x), span(h, DH)],
                      kv_send.at[a * group + h, j], kv_recv.at[a * group + h, j], at_z(up(j)))

    def kv_landing(a, h, j):
        place = pairs[a][1].at[frame(down(j), x), span(h, DH)]
        return remote(place, place, kv_send.at[a * group + h, j], kv_recv.at[a * group + h, j], at_z(down(j)))

    def x_copy(a, h, j):
        place = pairs[a][1].at[frame(down(j), x), span(h, DH)]
        source = place if j else pairs[a][0].at[:, span(z * group + h, DH)]
        return remote(source, place, x_send.at[a * group + h, j], x_recv.at[a * group + h, j], x_peer)

    def x_landing(a, h, j):
        place = pairs[a][1].at[frame(down(j), 1 - x), span(h, DH)]
        return remote(place, place, x_send.at[a * group + h, j], x_recv.at[a * group + h, j], x_peer)

    def part_of(unit, zz):
        u, start, size = unit
        return pl.ds(pl.multiple_of(start * nz + zz * size, size), size)

    def rows_of(unit):
        u, start, size = unit
        return pl.ds(pl.multiple_of(start, size), size)

    def q_copy(unit, j):
        return remote(q_ref.at[rows_of(unit), span(up(j), wide)], qbuf.at[part_of(unit, z), :],
                      q_send.at[unit[0], j], q_recv.at[unit[0], j], at_z(up(j)))

    def q_landing(unit, j):
        place = qbuf.at[part_of(unit, down(j)), :]
        return remote(place, place, q_send.at[unit[0], j], q_recv.at[unit[0], j], at_z(down(j)))

    def o_copy(unit, h, j):
        mark = unit[0] * group + h
        return remote(obuf.at[part_of(unit, up(j)), span(h, DH)], oin.at[rows_of(unit), span(z * group + h, DH)],
                      o_send.at[mark, j], o_recv.at[mark, j], at_z(up(j)))

    def o_landing(unit, h, j):
        mark = unit[0] * group + h
        place = oin.at[rows_of(unit), span(down(j) * group + h, DH)]
        return remote(place, place, o_send.at[mark, j], o_recv.at[mark, j], at_z(down(j)))

    def y_copy(unit, n):
        here = rows_of(unit)
        return remote(ysend.at[here, span(n, tile)], yrecv.at[here, span(n, tile)],
                      y_send.at[unit[0], n], y_recv.at[unit[0], n], y_peer)

    def own_kv(a):
        return pltpu.make_async_copy(pairs[a][0].at[:, span(z, wide)], pairs[a][1].at[frame(z, x), :], own_sem.at[a])

    def own_query(unit):
        return pltpu.make_async_copy(q_ref.at[rows_of(unit), span(z, wide)], qbuf.at[part_of(unit, z), :], own_q.at[unit[0]])

    def own_out(unit):
        return pltpu.make_async_copy(obuf.at[part_of(unit, z), :], oin.at[rows_of(unit), span(z, wide)], own_o.at[unit[0]])

    def out_copy(unit):
        here = rows_of(unit)
        return pltpu.make_async_copy(mine.at[here, :], out_ref.at[here, :], out_sem.at[unit[0]])

    def early_unit(c):
        return (c, c * BLK, BLK)

    cut = BLK // 2
    late = [(early + i, early * BLK + i * cut, cut) for i in range(2)]
    units = [early_unit(c) for c in range(early)] + late

    def send_queries(unit):
        for j in range(nz - 1, 0, -1):
            q_copy(unit, j).start()

    def send_head(h):
        for a in range(2):
            for j in range(nz - 1, 0, -1):
                kv_copy(a, h, j).start()
            x_copy(a, h, 0).start()

    send_queries(units[0])
    send_head(0)
    for c in range(1, early):
        send_queries(units[c])
    send_head(1)
    for a in range(2):
        own_kv(a).start()
    for unit in units:
        own_query(unit).start()

    key_block = lax.broadcasted_iota(jnp.int32, (1, bias.shape[1]), 1) // BLK

    @pl.loop(0, blocks * nz)
    def make_bias(i):
        c, zz = i // nz, lax.rem(i, nz)
        b = (zz * 2 + x) * blocks + c
        used = count_ref[b]
        line = jnp.full((1, bias.shape[1]), -1e30, jnp.float32)
        for s in range(slots):
            listed = jnp.where(s < used, list_ref[b, s], -1)
            line = jnp.where(key_block == listed, 0.0, line)
        bias[pl.ds(i, 1), :] = line

    def attend(query, key, value, lines):
        score = lax.dot_general(query, key, (((1,), (1,)), ((), ())), preferred_element_type=jnp.float32)
        if lines is not None:
            step = score.shape[0] // len(lines)
            score = jnp.concatenate(
                [score[i * step:(i + 1) * step] + line for i, line in enumerate(lines)], axis=0)
        top = jnp.max(score, axis=1, keepdims=True)
        weight = jnp.exp2((score - top) * factor)
        total = jnp.sum(weight, axis=1, keepdims=True)
        summed = jnp.dot(weight.astype(jnp.bfloat16), value, preferred_element_type=jnp.float32)
        return (summed / total).astype(jnp.bfloat16)

    @pl.loop(0, nz)
    def cross(g):
        cols = span(g, wide)
        parts = [pltpu.make_async_copy(src.at[:, cols], dst, c_sem.at[n])
                 for n, (src, dst) in enumerate(((cq_ref, cqb), (tk_ref, tkb), (tv_ref, tvb)))]
        for part in parts:
            part.start()
        for part in parts:
            part.wait()

        @pl.loop(0, group)
        def one(h):
            head = span(h, DH)
            cob[:, head] = attend(cqb[:, head], tkb[:, head], tvb[:, head], None)

        back = pltpu.make_async_copy(cob, cross_ref.at[:, cols], c_sem.at[3])
        back.start()
        back.wait()

    def attend_chunk(unit, block, h):
        u, start, size = unit
        head = span(h, DH)
        many = 2 * BLK // size
        for r in range(nz // many):
            lines = [bias[pl.ds(block * nz + many * r + i, 1), :] for i in range(many)]
            here = pl.ds(pl.multiple_of(start * nz + r * 2 * BLK, 2 * BLK), 2 * BLK)
            obuf[here, head] = attend(qbuf[here, head], kbuf[:, head], vbuf[:, head], lines)

    def wait_queries(unit):
        own_query(unit).wait()
        for j in range(1, nz):
            q_landing(unit, j).wait_recv()

    def project(unit):
        own_out(unit).wait()

        @pl.loop(0, group)
        def arrived(h):
            for j in range(1, nz):
                o_landing(unit, h, j).wait_recv()

        here = rows_of(unit)

        def product(base, n):
            cols = pl.ds(pl.multiple_of(base * half + n * tile, tile), tile)
            return jnp.dot(oin[here, :], wbuf[:, cols], preferred_element_type=jnp.float32).astype(jnp.bfloat16)

        @pl.loop(0, half // tile)
        def theirs(n):
            ysend[here, span(n, tile)] = product(1 - y, n)
            y_copy(unit, n).start()

        @pl.loop(0, half // tile)
        def ours(n):
            mine[here, span(n, tile)] = product(y, n)

    def finish(unit):
        here = rows_of(unit)

        @pl.loop(0, half // tile)
        def columns(n):
            y_copy(unit, n).wait_recv()
            cols = span(n, tile)
            mine[here, cols] = (mine[here, cols].astype(jnp.float32) + yrecv[here, cols].astype(jnp.float32)).astype(jnp.bfloat16)

        out_copy(unit).start()

    for a in range(2):
        own_kv(a).wait()

    def send_outputs(unit, h):
        for j in range(nz - 1, 0, -1):
            o_copy(unit, h, j).start()

    @pl.loop(0, group + 1)
    def arrive(h):
        @pl.when(h < group)
        def pass_on():
            for a in range(2):
                for j in range(nz - 1, 0, -1):
                    kv_landing(a, h, j).wait_recv()
                    x_copy(a, h, j).start()

        @pl.when(h + 2 < group)
        def more():
            send_head(h + 2)

        @pl.when(h == max(group - 2, 0))
        def last_queries():
            for unit in late:
                send_queries(unit)

        @pl.when(h == group)
        def first_outputs():
            @pl.loop(0, group - 1)
            def one(i):
                send_outputs(units[0], i)

        @pl.when(h == 1)
        def first_queries():
            for c in range(early):
                wait_queries(units[c])

        @pl.when(h >= 1)
        def compute():
            for a in range(2):
                for j in range(nz):
                    x_landing(a, h - 1, j).wait_recv()

            @pl.loop(0, early)
            def one(c):
                attend_chunk(early_unit(c), c, h - 1)

    @pl.loop(0, early)
    def give_back(c):
        own_out(early_unit(c)).start()

        @pl.loop(jnp.where(c == 0, group - 1, 0), group)
        def one(h):
            send_outputs(early_unit(c), h)

    own_w.wait()
    for i, unit in enumerate(late):
        wait_queries(unit)

        @pl.loop(0, group)
        def one(h):
            attend_chunk(unit, early, h)
            send_outputs(unit, h)

        own_out(unit).start()
        if i == 0:
            project(units[0])

    @pl.loop(1, early)
    def projected(c):
        project(early_unit(c))

    for unit in late:
        project(unit)

    for unit in units:
        finish(unit)

    for unit in units:
        out_copy(unit).wait()

        @pl.loop(0, half // tile)
        def one(n):
            y_copy(unit, n).wait_send()

        @pl.loop(0, group)
        def two(h):
            for j in range(1, nz):
                o_copy(unit, h, j).wait_send()

        for j in range(1, nz):
            q_copy(unit, j).wait_send()

    @pl.loop(0, group)
    def heads_sent(h):
        for a in range(2):
            for j in range(nz):
                x_copy(a, h, j).wait_send()
            for j in range(1, nz):
                kv_copy(a, h, j).wait_send()


def fused(nseq, queries, keys, values, cross_query, text_keys, text_values, out_weight, block_list, block_count):
    nz = nseq // 2
    rows, width = queries.shape
    heads_here = width // DH
    group = heads_here // nz
    wide = group * DH
    blocks = rows // BLK
    units = blocks + 1
    tokens = nseq * rows
    text = text_keys.shape[0]
    half = out_weight.shape[1] // 2
    bf = jnp.bfloat16
    dma = pltpu.SemaphoreType.DMA
    hbm = pl.BlockSpec(memory_space=pl.ANY)
    smem = pl.BlockSpec(memory_space=pltpu.SMEM)
    return pl.pallas_call(
        functools.partial(fused_kernel, (nz, rows, group, text, block_list.shape[1])),
        out_shape=(jax.ShapeDtypeStruct((rows, half), bf), jax.ShapeDtypeStruct((rows, width), bf)),
        in_specs=[hbm] * 7 + [smem] * 2,
        out_specs=(hbm, hbm),
        scratch_shapes=[
            pltpu.VMEM((tokens, wide), bf), pltpu.VMEM((tokens, wide), bf),
            pltpu.VMEM((nz * rows, wide), bf), pltpu.VMEM((nz * rows, wide), bf),
            pltpu.VMEM((rows, width), bf), pltpu.VMEM(out_weight.shape, bf),
            pltpu.VMEM((rows, half), bf), pltpu.VMEM((rows, half), bf), pltpu.VMEM((rows, half), bf),
            pltpu.VMEM((nz * blocks, tokens), jnp.float32),
            pltpu.VMEM((rows, wide), bf), pltpu.VMEM((text, wide), bf), pltpu.VMEM((text, wide), bf),
            pltpu.VMEM((rows, wide), bf),
            dma((2 * group, nz)), dma((2 * group, nz)), dma((2 * group, nz)), dma((2 * group, nz)),
            dma((units, nz)), dma((units, nz)), dma((units * group, nz)), dma((units * group, nz)),
            dma((units, half // 512)), dma((units, half // 512)), dma((3,)), dma((units,)), dma((units,)), dma((4,)), dma((units,)),
        ],
        compiler_params=pltpu.CompilerParams(
            collective_id=0, has_side_effects=True, vmem_limit_bytes=62 * 1024 * 1024),
        cost_estimate=pl.CostEstimate(
            flops=4 * rows * tokens * width + 4 * rows * width * half + 4 * rows * text * width,
            bytes_accessed=2 * (6 * rows * width + 2 * text * width + 2 * width * half),
            transcendentals=rows * heads_here * (tokens + text)),
    )(queries, keys, values, cross_query, text_keys, text_values, out_weight, block_list, block_count)


def solution(mesh):
    in_specs = (
        P(("pair", "seq"), "head"),
        P(("pair", "seq"), "head"),
        P(("pair", "seq"), "head"),
        P(("pair", "seq"), "head"),
        P("pair", "head"),
        P("pair", "head"),
        P("head", None),
        P(),
        P(),
    )
    out_specs = (P(("pair", "seq"), "head"), P(("pair", "seq"), "head"))
    nseq = mesh.shape["seq"]

    def choose(*args):
        width = args[0].shape[1]
        nz = nseq // 2
        fits = mesh.shape["head"] == 2 and nseq % 4 == 0 and (width // DH) % nz == 0 and width // DH >= 2 * nz
        return functools.partial(fused, nseq)(*args) if fits else body(*args)

    return jax.shard_map(choose, mesh=mesh, in_specs=in_specs, out_specs=out_specs, check_vma=False)
```

```python
import functools

import jax
import jax.numpy as jnp
from jax import lax
from jax.experimental import pallas as pl
from jax.experimental.pallas import tpu as pltpu
from jax.sharding import PartitionSpec as P

DH = 128
BLK = 128


def allowed_table(block_list, block_count):
    slots = jnp.arange(block_list.shape[1], dtype=jnp.int32)
    targets = jnp.arange(block_list.shape[0], dtype=jnp.int32)
    hit = (block_list[:, :, None] == targets[None, None, :]) & (
        slots[None, :, None] < block_count[:, None, None]
    )
    return jnp.any(hit, axis=1).astype(jnp.int32)


def attend_tile(carry, query_three, key_tile, value_tile, tile_mask, scale):
    row_max, total, summed = carry
    count = key_tile.shape[0]
    heads_here = query_three.shape[1]
    key_three = key_tile.reshape(count, heads_here, DH)
    value_three = value_tile.reshape(count, heads_here, DH)
    score = (
        jnp.einsum("qhd,khd->hqk", query_three, key_three, preferred_element_type=jnp.float32)
        * scale
    )
    score = jnp.where(tile_mask[None], score, -1e30)
    new_max = jnp.maximum(row_max, jnp.max(score, axis=2))
    weight = jnp.where(tile_mask[None], jnp.exp(score - new_max[:, :, None]), 0.0)
    factor = jnp.exp(row_max - new_max)
    total = total * factor + jnp.sum(weight, axis=2)
    update = jnp.einsum(
        "hqk,khd->hqd", weight.astype(jnp.bfloat16), value_three, preferred_element_type=jnp.float32
    )
    summed = summed * factor[:, :, None] + update
    return (new_max, total, summed)


def masked_update(carry, query_three, key_tile, value_tile, tile_mask, scale):
    return attend_tile(carry, query_three, key_tile, value_tile, tile_mask, scale)


def empty_state(heads_here, count):
    return (
        jnp.full((heads_here, count), -1e30, jnp.float32),
        jnp.zeros((heads_here, count), jnp.float32),
        jnp.zeros((heads_here, count, DH), jnp.float32),
    )


def body(
    queries, keys, values, cross_query, text_keys, text_values, out_weight, block_list, block_count
):
    scale = DH ** (-0.5)
    rows = queries.shape[0]
    heads_here = queries.shape[1] // DH
    blocks_here = rows // BLK
    allowed = allowed_table(block_list, block_count) > 0
    my_first = lax.axis_index("seq") * blocks_here
    query_three = queries.reshape(rows, heads_here, DH)
    row_allowed = jnp.repeat(
        lax.dynamic_slice_in_dim(allowed, my_first, blocks_here, 0), BLK, axis=0
    )
    key_piece = lax.all_gather(keys, "seq", axis=0, tiled=True)
    value_piece = lax.all_gather(values, "seq", axis=0, tiled=True)
    count = key_piece.shape[0]
    shards_in = count // rows
    factor = 1
    for candidate in range(1, shards_in + 1):
        if shards_in % candidate == 0 and candidate * rows <= 1536:
            factor = candidate
    width = factor * rows
    piece_mask = jnp.repeat(row_allowed, BLK, axis=1)
    tiles = count // width
    key_tiles = key_piece.reshape(tiles, width, key_piece.shape[1])
    value_tiles = value_piece.reshape(tiles, width, value_piece.shape[1])
    mask_tiles = piece_mask.reshape(rows, tiles, width).transpose(1, 0, 2)

    def step(state, items):
        return (masked_update(state, query_three, items[0], items[1], items[2], scale), None)

    state, unused = lax.scan(
        step, empty_state(heads_here, rows), (key_tiles, value_tiles, mask_tiles)
    )
    row_max, total, summed = state
    self_three = (summed / total[:, :, None]).transpose(1, 0, 2)
    self_heads = self_three.reshape(rows, heads_here * DH).astype(jnp.bfloat16)
    term = jnp.dot(self_heads, out_weight, preferred_element_type=jnp.float32)
    block_stream = lax.psum_scatter(
        term.astype(jnp.bfloat16), "head", scatter_dimension=1, tiled=True
    )
    cross_three = cross_query.reshape(rows, heads_here, DH)
    text_count = text_keys.shape[0]
    text_key_three = text_keys.reshape(text_count, heads_here, DH)
    text_value_three = text_values.reshape(text_count, heads_here, DH)
    cross_score = (
        jnp.einsum("qhd,khd->hqk", cross_three, text_key_three, preferred_element_type=jnp.float32)
        * scale
    )
    cross_max = jnp.max(cross_score, axis=2, keepdims=True)
    cross_weight = jnp.exp(cross_score - cross_max)
    cross_total = jnp.sum(cross_weight, axis=2)
    cross_sum = jnp.einsum(
        "hqk,khd->hqd",
        cross_weight.astype(jnp.bfloat16),
        text_value_three,
        preferred_element_type=jnp.float32,
    )
    cross_heads = (
        (cross_sum / cross_total[:, :, None])
        .transpose(1, 0, 2)
        .reshape(rows, heads_here * DH)
        .astype(jnp.bfloat16)
    )
    return (block_stream, cross_heads)


def fused_kernel(
    sizes,
    q_ref, k_ref, v_ref, cq_ref, tk_ref, tv_ref, w_ref, list_ref, count_ref,
    out_ref, cross_ref,
    kbuf, vbuf, qbuf, obuf, oin, wbuf, mine, ysend, yrecv, bias, cqb, tkb, tvb, cob,
    kv_send, kv_recv, x_send, x_recv, q_send, q_recv, o_send, o_recv, y_send, y_recv, own_sem, own_q, own_o, c_sem, out_sem,
):
    nz, rows, group, text, slots = sizes
    wide = group * DH
    blocks = rows // BLK
    chunk = nz * BLK
    half = out_ref.shape[1]
    seq = lax.axis_index("seq")
    z, x = seq // 2, lax.rem(seq, 2)
    y = lax.axis_index("head")
    tile = 512
    factor = (DH ** (-0.5)) * 1.4426950408889634

    def at_z(zz):
        return {"seq": zz * 2 + x}

    def up(j):
        return lax.rem(z + j, nz)

    def down(j):
        return lax.rem(z + nz - j, nz)

    x_peer = {"seq": z * 2 + 1 - x}
    y_peer = {"head": 1 - y}

    def span(i, size):
        return pl.ds(pl.multiple_of(i * size, size), size)

    def remote(src, dst, send, recv, where):
        return pltpu.make_async_remote_copy(
            src_ref=src, dst_ref=dst, send_sem=send, recv_sem=recv,
            device_id=where, device_id_type=pl.DeviceIdType.MESH,
        )

    def frame(zz, xx):
        return span(zz * 2 + xx, rows)

    own_w = pltpu.make_async_copy(w_ref, wbuf, own_sem.at[2])
    own_w.start()

    barrier = pltpu.get_barrier_semaphore()
    for j in range(1, nz):
        pl.semaphore_signal(barrier, inc=1, device_id=at_z(up(j)), device_id_type=pl.DeviceIdType.MESH)
    pl.semaphore_signal(barrier, inc=1, device_id=x_peer, device_id_type=pl.DeviceIdType.MESH)
    pl.semaphore_signal(barrier, inc=1, device_id=y_peer, device_id_type=pl.DeviceIdType.MESH)
    pl.semaphore_wait(barrier, nz + 1)

    pairs = ((k_ref, kbuf), (v_ref, vbuf))
    early = blocks - 1

    def kv_copy(a, h, j):
        return remote(pairs[a][0].at[:, span(up(j) * group + h, DH)], pairs[a][1].at[frame(z, x), span(h, DH)],
                      kv_send.at[a * group + h, j], kv_recv.at[a * group + h, j], at_z(up(j)))

    def kv_landing(a, h, j):
        place = pairs[a][1].at[frame(down(j), x), span(h, DH)]
        return remote(place, place, kv_send.at[a * group + h, j], kv_recv.at[a * group + h, j], at_z(down(j)))

    def x_copy(a, h, j):
        place = pairs[a][1].at[frame(down(j), x), span(h, DH)]
        source = place if j else pairs[a][0].at[:, span(z * group + h, DH)]
        return remote(source, place, x_send.at[a * group + h, j], x_recv.at[a * group + h, j], x_peer)

    def x_landing(a, h, j):
        place = pairs[a][1].at[frame(down(j), 1 - x), span(h, DH)]
        return remote(place, place, x_send.at[a * group + h, j], x_recv.at[a * group + h, j], x_peer)

    def part_of(unit, zz):
        u, start, size = unit
        return pl.ds(pl.multiple_of(start * nz + zz * size, size), size)

    def rows_of(unit):
        u, start, size = unit
        return pl.ds(pl.multiple_of(start, size), size)

    def q_copy(unit, j):
        return remote(q_ref.at[rows_of(unit), span(up(j), wide)], qbuf.at[part_of(unit, z), :],
                      q_send.at[unit[0], j], q_recv.at[unit[0], j], at_z(up(j)))

    def q_landing(unit, j):
        place = qbuf.at[part_of(unit, down(j)), :]
        return remote(place, place, q_send.at[unit[0], j], q_recv.at[unit[0], j], at_z(down(j)))

    def o_copy(unit, h, j):
        mark = unit[0] * group + h
        return remote(obuf.at[part_of(unit, up(j)), span(h, DH)], oin.at[rows_of(unit), span(z * group + h, DH)],
                      o_send.at[mark, j], o_recv.at[mark, j], at_z(up(j)))

    def o_landing(unit, h, j):
        mark = unit[0] * group + h
        place = oin.at[rows_of(unit), span(down(j) * group + h, DH)]
        return remote(place, place, o_send.at[mark, j], o_recv.at[mark, j], at_z(down(j)))

    def y_copy(unit, n):
        here = rows_of(unit)
        return remote(ysend.at[here, span(n, tile)], yrecv.at[here, span(n, tile)],
                      y_send.at[unit[0], n], y_recv.at[unit[0], n], y_peer)

    def own_kv(a):
        return pltpu.make_async_copy(pairs[a][0].at[:, span(z, wide)], pairs[a][1].at[frame(z, x), :], own_sem.at[a])

    def own_query(unit):
        return pltpu.make_async_copy(q_ref.at[rows_of(unit), span(z, wide)], qbuf.at[part_of(unit, z), :], own_q.at[unit[0]])

    def own_out(unit):
        return pltpu.make_async_copy(obuf.at[part_of(unit, z), :], oin.at[rows_of(unit), span(z, wide)], own_o.at[unit[0]])

    def out_copy(unit):
        here = rows_of(unit)
        return pltpu.make_async_copy(mine.at[here, :], out_ref.at[here, :], out_sem.at[unit[0]])

    def early_unit(c):
        return (c, c * BLK, BLK)

    cut = BLK // 2
    late = [(early + i, early * BLK + i * cut, cut) for i in range(2)]
    units = [early_unit(c) for c in range(early)] + late

    def send_queries(unit):
        for j in range(nz - 1, 0, -1):
            q_copy(unit, j).start()

    def send_head(h):
        for a in range(2):
            for j in range(nz - 1, 0, -1):
                kv_copy(a, h, j).start()
            x_copy(a, h, 0).start()

    send_queries(units[0])
    send_head(0)
    for c in range(1, early):
        send_queries(units[c])
    send_head(1)
    for a in range(2):
        own_kv(a).start()
    for unit in units:
        own_query(unit).start()

    key_block = lax.broadcasted_iota(jnp.int32, (1, bias.shape[1]), 1) // BLK

    @pl.loop(0, blocks * nz)
    def make_bias(i):
        c, zz = i // nz, lax.rem(i, nz)
        b = (zz * 2 + x) * blocks + c
        used = count_ref[b]
        line = jnp.full((1, bias.shape[1]), -1e30, jnp.float32)
        for s in range(slots):
            listed = jnp.where(s < used, list_ref[b, s], -1)
            line = jnp.where(key_block == listed, 0.0, line)
        bias[pl.ds(i, 1), :] = line

    def attend(query, key, value, lines):
        score = lax.dot_general(query, key, (((1,), (1,)), ((), ())), preferred_element_type=jnp.float32)
        if lines is not None:
            step = score.shape[0] // len(lines)
            score = jnp.concatenate(
                [score[i * step:(i + 1) * step] + line for i, line in enumerate(lines)], axis=0)
        top = jnp.max(score, axis=1, keepdims=True)
        weight = jnp.exp2((score - top) * factor)
        total = jnp.sum(weight, axis=1, keepdims=True)
        summed = jnp.dot(weight.astype(jnp.bfloat16), value, preferred_element_type=jnp.float32)
        return (summed / total).astype(jnp.bfloat16)

    @pl.loop(0, nz)
    def cross(g):
        cols = span(g, wide)
        parts = [pltpu.make_async_copy(src.at[:, cols], dst, c_sem.at[n])
                 for n, (src, dst) in enumerate(((cq_ref, cqb), (tk_ref, tkb), (tv_ref, tvb)))]
        for part in parts:
            part.start()
        for part in parts:
            part.wait()

        @pl.loop(0, group)
        def one(h):
            head = span(h, DH)
            cob[:, head] = attend(cqb[:, head], tkb[:, head], tvb[:, head], None)

        back = pltpu.make_async_copy(cob, cross_ref.at[:, cols], c_sem.at[3])
        back.start()
        back.wait()

    def attend_chunk(unit, block, h):
        u, start, size = unit
        head = span(h, DH)
        many = 2 * BLK // size
        for r in range(nz // many):
            lines = [bias[pl.ds(block * nz + many * r + i, 1), :] for i in range(many)]
            here = pl.ds(pl.multiple_of(start * nz + r * 2 * BLK, 2 * BLK), 2 * BLK)
            obuf[here, head] = attend(qbuf[here, head], kbuf[:, head], vbuf[:, head], lines)

    def wait_queries(unit):
        own_query(unit).wait()
        for j in range(1, nz):
            q_landing(unit, j).wait_recv()

    def project(unit):
        own_out(unit).wait()

        @pl.loop(0, group)
        def arrived(h):
            for j in range(1, nz):
                o_landing(unit, h, j).wait_recv()

        here = rows_of(unit)

        def product(base, n):
            cols = pl.ds(pl.multiple_of(base * half + n * tile, tile), tile)
            return jnp.dot(oin[here, :], wbuf[:, cols], preferred_element_type=jnp.float32).astype(jnp.bfloat16)

        @pl.loop(0, half // tile)
        def theirs(n):
            ysend[here, span(n, tile)] = product(1 - y, n)
            y_copy(unit, n).start()

        @pl.loop(0, half // tile)
        def ours(n):
            mine[here, span(n, tile)] = product(y, n)

    def finish(unit):
        here = rows_of(unit)

        @pl.loop(0, half // tile)
        def columns(n):
            y_copy(unit, n).wait_recv()
            cols = span(n, tile)
            mine[here, cols] = (mine[here, cols].astype(jnp.float32) + yrecv[here, cols].astype(jnp.float32)).astype(jnp.bfloat16)

        out_copy(unit).start()

    for a in range(2):
        own_kv(a).wait()

    def send_outputs(unit, h):
        for j in range(nz - 1, 0, -1):
            o_copy(unit, h, j).start()

    @pl.loop(0, group + 1)
    def arrive(h):
        @pl.when(h < group)
        def pass_on():
            for a in range(2):
                for j in range(nz - 1, 0, -1):
                    kv_landing(a, h, j).wait_recv()
                    x_copy(a, h, j).start()

        @pl.when(h + 2 < group)
        def more():
            send_head(h + 2)

        @pl.when(h == max(group - 2, 0))
        def last_queries():
            for unit in late:
                send_queries(unit)

        @pl.when(h == group)
        def first_outputs():
            @pl.loop(0, group - 1)
            def one(i):
                send_outputs(units[0], i)

        @pl.when(h == 1)
        def first_queries():
            for c in range(early):
                wait_queries(units[c])

        @pl.when(h >= 1)
        def compute():
            for a in range(2):
                for j in range(nz):
                    x_landing(a, h - 1, j).wait_recv()

            @pl.loop(0, early)
            def one(c):
                attend_chunk(early_unit(c), c, h - 1)

                @pl.when(h == group)
                def give_back():
                    own_out(early_unit(c)).start()

                    @pl.loop(jnp.where(c == 0, group - 1, 0), group)
                    def each(i):
                        send_outputs(early_unit(c), i)

    own_w.wait()
    for i, unit in enumerate(late):
        wait_queries(unit)

        @pl.loop(0, group)
        def one(h):
            attend_chunk(unit, early, h)
            send_outputs(unit, h)

        own_out(unit).start()
        if i == 0:
            project(units[0])

    @pl.loop(1, early)
    def projected(c):
        project(early_unit(c))

    for unit in late:
        project(unit)

    for unit in units:
        finish(unit)

    for unit in units:
        out_copy(unit).wait()

        @pl.loop(0, half // tile)
        def one(n):
            y_copy(unit, n).wait_send()

        @pl.loop(0, group)
        def two(h):
            for j in range(1, nz):
                o_copy(unit, h, j).wait_send()

        for j in range(1, nz):
            q_copy(unit, j).wait_send()

    @pl.loop(0, group)
    def heads_sent(h):
        for a in range(2):
            for j in range(nz):
                x_copy(a, h, j).wait_send()
            for j in range(1, nz):
                kv_copy(a, h, j).wait_send()


def fused(nseq, queries, keys, values, cross_query, text_keys, text_values, out_weight, block_list, block_count):
    nz = nseq // 2
    rows, width = queries.shape
    heads_here = width // DH
    group = heads_here // nz
    wide = group * DH
    blocks = rows // BLK
    units = blocks + 1
    tokens = nseq * rows
    text = text_keys.shape[0]
    half = out_weight.shape[1] // 2
    bf = jnp.bfloat16
    dma = pltpu.SemaphoreType.DMA
    hbm = pl.BlockSpec(memory_space=pl.ANY)
    smem = pl.BlockSpec(memory_space=pltpu.SMEM)
    return pl.pallas_call(
        functools.partial(fused_kernel, (nz, rows, group, text, block_list.shape[1])),
        out_shape=(jax.ShapeDtypeStruct((rows, half), bf), jax.ShapeDtypeStruct((rows, width), bf)),
        in_specs=[hbm] * 7 + [smem] * 2,
        out_specs=(hbm, hbm),
        scratch_shapes=[
            pltpu.VMEM((tokens, wide), bf), pltpu.VMEM((tokens, wide), bf),
            pltpu.VMEM((nz * rows, wide), bf), pltpu.VMEM((nz * rows, wide), bf),
            pltpu.VMEM((rows, width), bf), pltpu.VMEM(out_weight.shape, bf),
            pltpu.VMEM((rows, half), bf), pltpu.VMEM((rows, half), bf), pltpu.VMEM((rows, half), bf),
            pltpu.VMEM((nz * blocks, tokens), jnp.float32),
            pltpu.VMEM((rows, wide), bf), pltpu.VMEM((text, wide), bf), pltpu.VMEM((text, wide), bf),
            pltpu.VMEM((rows, wide), bf),
            dma((2 * group, nz)), dma((2 * group, nz)), dma((2 * group, nz)), dma((2 * group, nz)),
            dma((units, nz)), dma((units, nz)), dma((units * group, nz)), dma((units * group, nz)),
            dma((units, half // 512)), dma((units, half // 512)), dma((3,)), dma((units,)), dma((units,)), dma((4,)), dma((units,)),
        ],
        compiler_params=pltpu.CompilerParams(
            collective_id=0, has_side_effects=True, vmem_limit_bytes=62 * 1024 * 1024),
        cost_estimate=pl.CostEstimate(
            flops=4 * rows * tokens * width + 4 * rows * width * half + 4 * rows * text * width,
            bytes_accessed=2 * (6 * rows * width + 2 * text * width + 2 * width * half),
            transcendentals=rows * heads_here * (tokens + text)),
    )(queries, keys, values, cross_query, text_keys, text_values, out_weight, block_list, block_count)


def solution(mesh):
    in_specs = (
        P(("pair", "seq"), "head"),
        P(("pair", "seq"), "head"),
        P(("pair", "seq"), "head"),
        P(("pair", "seq"), "head"),
        P("pair", "head"),
        P("pair", "head"),
        P("head", None),
        P(),
        P(),
    )
    out_specs = (P(("pair", "seq"), "head"), P(("pair", "seq"), "head"))
    nseq = mesh.shape["seq"]

    def choose(*args):
        width = args[0].shape[1]
        nz = nseq // 2
        fits = mesh.shape["head"] == 2 and nseq % 4 == 0 and (width // DH) % nz == 0 and width // DH >= 2 * nz
        return functools.partial(fused, nseq)(*args) if fits else body(*args)

    return jax.shard_map(choose, mesh=mesh, in_specs=in_specs, out_specs=out_specs, check_vma=False)
```
